32 devices in a mesh: groups: 2 (over y), outer: 4 (over x, core), inner: 4 (over z).
Axes of the slice: x: 2, y: 2, z: 4, core: 2. Of those that a mesh axis runs over, the one named last changes fastest.
Arguments:
- hidden: bfloat16 [12288, 3584], P(('groups', 'outer', 'inner')), parts along dimension 0, may hold values from -27 to 27
- gain: float32 [3584], replicated, may hold values from 0.5 to 9
- w_qkv: bfloat16 [3584, 2304], P('outer'), may hold values from -0.09375 to 0.09375
- bias: float32 [2304], replicated, may hold values from -4 to 4
- boundaries: int32 [132], P('groups'), parts along dimension 0, may hold values from 0 to 6144, as said below
- loader_counts: int32 [8, 4, 4], P('groups'), parts along dimension 0, may hold values from 48 to 144, as said below
Outputs:
- attended: bfloat16 [12288, 1792], P(('groups', 'outer', 'inner')), parts along dimension 0
The draws below stay inside these ranges and needn't reach their ends.
There are 2 independent parts, one for each index of `groups`. The reference program is written for one: setup_inputs(seed, part) draws one part's arguments, and reference() takes and returns one part's arrays. A program takes and returns all parts, laid end to end along the dimension named above; an argument that names none is the same for every part. Nothing has to cross between parts.
Inputs may be any that keep to these rules, and one draw needn't show every extreme that they name: `boundaries`: starts at 0, never falls, and ends at 6144. Every document has at most 1536 tokens and one has exactly 1536; all but the last nonempty one have at least 96; trailing entries equal 6144. In every node, each row and each column of loader_counts[k] sums to 384, and some entry equals 144.
All inputs are finite; a program needn't handle non-finite values.
Results may differ from the reference program's by a relative error of at most 0.02.
The reference program's roundings to bfloat16 on the way count: a program that leaves them out, or rounds other values in their place, can miss the bound.
Values may be sent and summed in bfloat16 or wider, within the bound.
No kernel may reach another device: no remote copies, remote signals or barrier semaphores. Data moves between devices by JAX's collectives and lax.ppermute only.
A program may use at most 128 MiB of HBM per device.

```python
import math
import jax
import jax.numpy as jnp
from jax import lax

D = 3584
HEAD_SIZE = 128
HQ = 14
KEY_VALUE_HEADS = 2
DEVICE_TOKENS = 384
SPAN = 4
QKV = 2304
QUERY_PER_KEY = 7
NODES = 4
NODE_DEVS = 4
PACKED_TOKENS = 6144
DOC_MOST = 1536
DOC_LEAST = 96
MAXDOCS = 65
SHARE = 96


def draw_hidden(key, part):
    noise_key, row_key, column_key = jax.random.split(key, 3)
    row_scale = jnp.exp(jax.random.uniform(row_key, (PACKED_TOKENS, 1), jnp.float32, jnp.log(0.3), jnp.log(3.0)))
    column_scale = jnp.exp(jax.random.uniform(column_key, (1, D), jnp.float32, jnp.log(0.3), jnp.log(3.0)))
    signal = jnp.clip(jax.random.normal(noise_key, (PACKED_TOKENS, D), jnp.float32), -3.0, 3.0)
    return (signal * row_scale * column_scale).astype(jnp.bfloat16)


def draw_gain(key, part):
    result = jnp.exp(jax.random.uniform(key, (D,), jnp.float32, jnp.log(0.5), jnp.log(2.0)))
    return result.astype(jnp.float32)


def draw_boundaries(key, part):
    length_key, place_key = jax.random.split(key, 2)
    lengths = jax.random.randint(length_key, (MAXDOCS,), DOC_LEAST, DOC_MOST + 1, dtype=jnp.int32)
    longest = jax.random.randint(place_key, (), 0, PACKED_TOKENS // DOC_MOST, dtype=jnp.int32)
    lengths = jnp.where(jnp.arange(MAXDOCS, dtype=jnp.int32) == longest, DOC_MOST, lengths)
    doc_ends = jnp.minimum(jnp.cumsum(lengths).astype(jnp.int32), PACKED_TOKENS)
    return jnp.concatenate([jnp.zeros((1,), jnp.int32), doc_ends]).astype(jnp.int32)


def draw_loader_counts(key, part):

    def one_node(node_key):
        order_key, first_key, second_key, share_key = jax.random.split(node_key, 4)
        order = jax.random.permutation(order_key, NODE_DEVS).astype(jnp.int32)
        shift_one = jax.random.randint(first_key, (), 1, NODE_DEVS, dtype=jnp.int32)
        other = jax.random.randint(second_key, (), 1, NODE_DEVS - 1, dtype=jnp.int32)
        shift_two = jnp.where(other >= shift_one, other + 1, other)
        extra_one = jax.random.randint(share_key, (), 0, SHARE // 2 + 1, dtype=jnp.int32)
        extra_two = SHARE // 2 - extra_one
        senders = jnp.arange(NODE_DEVS, dtype=jnp.int32)
        raised = (order[:, None] == senders[None, :]).astype(jnp.int32)
        lower_one = (order[(senders + shift_one) % NODE_DEVS][:, None] == senders[None, :]).astype(jnp.int32)
        lower_two = (order[(senders + shift_two) % NODE_DEVS][:, None] == senders[None, :]).astype(jnp.int32)
        return (SHARE + (extra_one + extra_two) * raised - extra_one * lower_one - extra_two * lower_two).astype(jnp.int32)
    return jax.vmap(one_node)(jax.random.split(key, NODES)).astype(jnp.int32)


def levels(own_key, shape, cuts, least, high):
    def one(dim, shards_of):
        heights = jax.random.uniform(jax.random.fold_in(jax.random.fold_in(own_key, 6), dim), (shards_of,), jnp.float32, least / len(cuts), high / len(cuts))
        return jnp.repeat(jnp.exp(heights), shape[dim] // shards_of).reshape((-1,) + (1,) * (len(shape) - dim - 1))

    level = one(*cuts[0])
    for cut in cuts[1:]:
        level = level * one(*cut)
    return level


def gaussian(stream_key, shape, spread, most, cuts=(), kind=jnp.bfloat16):
    level = levels(stream_key, shape, cuts, -0.22, 0.18) if cuts else 1.0
    values = jax.random.normal(stream_key, shape, jnp.float32) * spread * level
    return jnp.minimum(jnp.maximum(values, -most), most).astype(kind)


def setup_inputs(seed: int = 0, part: int = 0) -> dict:
    streams_of = jax.random.split(jax.random.key(seed), 7)
    own_keys = jax.random.split(jax.random.fold_in(streams_of[6], part), 7)
    hidden = draw_hidden(jax.random.fold_in(jax.random.fold_in(streams_of[6], part), 71), part)
    gain = draw_gain(jax.random.fold_in(streams_of[6], 71), part)
    w_qkv = gaussian(streams_of[2], (D, QKV), D ** -0.5, 0.09375, ((0, 4),))
    bias = gaussian(streams_of[3], (QKV,), 1.0, 4.0, (), jnp.float32)
    boundaries = draw_boundaries(jax.random.fold_in(jax.random.fold_in(streams_of[6], part), 71), part)
    loader_counts = draw_loader_counts(jax.random.fold_in(jax.random.fold_in(streams_of[6], part), 71), part)
    return dict(hidden=hidden, gain=gain, w_qkv=w_qkv, bias=bias, boundaries=boundaries, loader_counts=loader_counts)


EPSILON = 1e-06
ROPE_BASE = 1000000.0
SCORE_MASKED = -1e+30

def source_rows(loader_counts):
    own_incl = jnp.cumsum(loader_counts, axis=1).astype(jnp.int32)
    own_excl = (own_incl - loader_counts).astype(jnp.int32)
    load_excl = (jnp.cumsum(loader_counts, axis=2) - loader_counts).astype(jnp.int32)
    own_incl_t = jnp.transpose(own_incl, (0, 2, 1))
    packed = jnp.arange(PACKED_TOKENS, dtype=jnp.int32)
    node_index = packed // (NODE_DEVS * DEVICE_TOKENS)
    owner = packed // DEVICE_TOKENS % NODE_DEVS
    inside = packed % DEVICE_TOKENS
    limits = own_incl_t[node_index, owner]
    sender = lax.optimization_barrier(jnp.sum((limits <= inside[:, None]).astype(jnp.int32), axis=1)).astype(jnp.int32)
    offset = own_excl[node_index, sender, owner]
    loader_start = load_excl[node_index, sender, owner]
    result = node_index * NODE_DEVS * DEVICE_TOKENS + sender * DEVICE_TOKENS + loader_start + inside - offset
    return result.astype(jnp.int32)

def doc_info(boundaries, token_positions):
    doc_ends = boundaries[1:]
    lengths = doc_ends - boundaries[:-1]
    passed = doc_ends[None, :] <= token_positions[:, None]
    doc_index = lax.optimization_barrier(jnp.sum(passed.astype(jnp.int32), axis=1)).astype(jnp.int32)
    doc_start = lax.optimization_barrier(jnp.sum(jnp.where(passed, lengths[None, :], 0), axis=1)).astype(jnp.int32)
    return (doc_index, doc_start)

def rotary_embed(rows_per_head, token_positions):
    width = rows_per_head.shape[-1]
    half_width = width // 2
    frequency = ROPE_BASE ** (-(jnp.arange(half_width, dtype=jnp.float32) * 2.0 / width))
    angles = token_positions.astype(jnp.float32)[:, None] * frequency[None, :]
    cosine = jnp.cos(angles)[:, None, :]
    sine_part = jnp.sin(angles)[:, None, :]
    first_half = rows_per_head[..., :half_width]
    second_half = rows_per_head[..., half_width:]
    return jnp.concatenate([first_half * cosine - second_half * sine_part, second_half * cosine + first_half * sine_part], axis=-1)

def reference(hidden, gain, w_qkv, bias, boundaries, loader_counts):
    rows_from = source_rows(loader_counts)
    gathered = jnp.take(hidden, rows_from, axis=0)
    widened = gathered.astype(jnp.float32)
    normed = (widened * lax.rsqrt(lax.optimization_barrier(jnp.mean(widened * widened, axis=1, keepdims=True)) + EPSILON) * gain).astype(jnp.bfloat16)
    projected_rows = jnp.dot(normed, w_qkv, preferred_element_type=jnp.float32) + bias
    packed = jnp.arange(PACKED_TOKENS, dtype=jnp.int32)
    doc_index, doc_start = doc_info(boundaries, packed)
    token_position = packed - doc_start
    width_of_query = HQ * HEAD_SIZE
    width_of_key = KEY_VALUE_HEADS * HEAD_SIZE
    query_rows = rotary_embed(projected_rows[:, :width_of_query].reshape(PACKED_TOKENS, HQ, HEAD_SIZE), token_position).astype(jnp.bfloat16)
    heads_for_key = rotary_embed(projected_rows[:, width_of_query:width_of_query + width_of_key].reshape(PACKED_TOKENS, KEY_VALUE_HEADS, HEAD_SIZE), token_position).astype(jnp.bfloat16)
    value_rows = projected_rows[:, width_of_query + width_of_key:].astype(jnp.bfloat16).reshape(PACKED_TOKENS, KEY_VALUE_HEADS, HEAD_SIZE)
    reachable_rows = SPAN * DEVICE_TOKENS
    window = reachable_rows + DEVICE_TOKENS
    padded_key_rows = jnp.concatenate([jnp.zeros((reachable_rows, KEY_VALUE_HEADS, HEAD_SIZE), jnp.bfloat16), heads_for_key], axis=0)
    padded_value_rows = jnp.concatenate([jnp.zeros((reachable_rows, KEY_VALUE_HEADS, HEAD_SIZE), jnp.bfloat16), value_rows], axis=0)
    docs_padded = jnp.concatenate([jnp.full((reachable_rows,), -1, jnp.int32), doc_index], axis=0)
    factor = 1.0 / math.sqrt(HEAD_SIZE)

    def block(block_index):
        starting_row = (block_index * DEVICE_TOKENS).astype(jnp.int32)
        block_of_queries = lax.dynamic_slice_in_dim(query_rows, starting_row, DEVICE_TOKENS, 0).astype(jnp.float32).reshape(DEVICE_TOKENS, KEY_VALUE_HEADS, QUERY_PER_KEY, HEAD_SIZE)
        block_of_keys = lax.dynamic_slice_in_dim(padded_key_rows, starting_row, window, 0).astype(jnp.float32)
        value_block = lax.dynamic_slice_in_dim(padded_value_rows, starting_row, window, 0).astype(jnp.float32)
        key_docs = lax.dynamic_slice_in_dim(docs_padded, starting_row, window, 0)
        query_docs = lax.dynamic_slice_in_dim(doc_index, starting_row, DEVICE_TOKENS, 0)
        query_pos = starting_row + jnp.arange(DEVICE_TOKENS, dtype=jnp.int32)
        key_pos = starting_row - reachable_rows + jnp.arange(window, dtype=jnp.int32)
        allowed = (query_docs[:, None] == key_docs[None, :]) & (key_pos[None, :] <= query_pos[:, None])
        scores = jnp.einsum('qkgd,lkd->kgql', block_of_queries, block_of_keys) * factor
        scores = jnp.where(allowed[None, None], scores, SCORE_MASKED)
        highest = lax.optimization_barrier(jnp.max(scores, axis=-1, keepdims=True))
        weights = jnp.where(allowed[None, None], jnp.exp(scores - highest), 0.0)
        running_sum = lax.optimization_barrier(jnp.sum(weights, axis=-1))
        rounded = lax.optimization_barrier(weights.astype(jnp.bfloat16)).astype(jnp.float32)
        output = jnp.einsum('kgql,lkd->qkgd', rounded, value_block, precision=lax.Precision.HIGHEST)
        output = output / jnp.transpose(running_sum, (2, 0, 1))[..., None]
        return output.reshape(DEVICE_TOKENS, HQ * HEAD_SIZE).astype(jnp.bfloat16)
    blocks = lax.map(block, jnp.arange(PACKED_TOKENS // DEVICE_TOKENS, dtype=jnp.int32))
    return blocks.reshape(PACKED_TOKENS, HQ * HEAD_SIZE)
```

```python
import functools
import math

import jax
import jax.numpy as jnp
from jax import lax
from jax.experimental import pallas as pl
from jax.experimental.pallas import tpu as pltpu
from jax.sharding import PartitionSpec as P

HEAD_SIZE = 128
HQ = 14
KEY_VALUE_HEADS = 2
QUERY_PER_KEY = 7
EPSILON = 1e-06
ROPE_BASE = 1000000.0
LEAST = -1e30
MASKED = -2e30
WIDTH_Q = HQ * HEAD_SIZE
WIDTH_K = KEY_VALUE_HEADS * HEAD_SIZE
TILE = 2 * HEAD_SIZE
CHUNKS = (8, 6)
VMEM_LIMIT = 40 * 1024 * 1024


def shifted(array, axis, by):
    length = lax.axis_size(axis)
    return lax.ppermute(array, axis, [(i, (i + by) % length) for i in range(length)])


def swapped(array, axis):
    length = lax.axis_size(axis)
    return lax.ppermute(array, axis, [(i, i ^ 1) for i in range(length)])


def from_behind(array, axis):
    length = lax.axis_size(axis)
    return lax.ppermute(array, axis, [(i, i + 1) for i in range(length - 1)])


def doc_starts(boundaries, token_positions):
    doc_ends = boundaries[1:]
    lengths = doc_ends - boundaries[:-1]
    passed = doc_ends[None, :] <= token_positions[:, None]
    return jnp.sum(jnp.where(passed, lengths[None, :], 0), axis=1)


def smem():
    return pl.BlockSpec(memory_space=pltpu.SMEM)


def whole_block(shape):
    return pl.BlockSpec(shape, lambda *_: (0,) * len(shape))


def norm_kernel(x_ref, gain_ref, out_ref):
    x = x_ref[...].astype(jnp.float32)
    scale = lax.rsqrt(jnp.mean(x * x, axis=1, keepdims=True) + EPSILON)
    y = (x * scale * gain_ref[...]).astype(jnp.bfloat16)
    depth = out_ref.shape[2]
    for k in range(out_ref.shape[0]):
        out_ref[k] = y[:, k * depth : (k + 1) * depth]


def normalize(hidden, gain, pieces):
    rows, features = hidden.shape
    step = rows // 3
    return pl.pallas_call(
        norm_kernel,
        grid=(rows // step,),
        in_specs=[
            pl.BlockSpec((step, features), lambda r: (r, 0)),
            whole_block((1, features)),
        ],
        out_specs=pl.BlockSpec((pieces, step, features // pieces), lambda r: (0, r, 0)),
        out_shape=jax.ShapeDtypeStruct((pieces, rows, features // pieces), jnp.bfloat16),
        compiler_params=pltpu.CompilerParams(vmem_limit_bytes=VMEM_LIMIT),
        cost_estimate=pl.CostEstimate(
            flops=4 * rows * features, bytes_accessed=4 * rows * features, transcendentals=rows
        ),
    )(hidden, gain[None])


def rotate(tile, cosine, sine):
    parts = []
    for h in range(tile.shape[1] // HEAD_SIZE):
        x = tile[:, h * HEAD_SIZE : (h + 1) * HEAD_SIZE]
        parts.append(x * cosine + pltpu.roll(x, HEAD_SIZE // 2, 1) * sine)
    return jnp.concatenate(parts, axis=1)


def send_start(counts, node, loader, owner, length):
    total = jnp.int32(0)
    for d in range(length):
        total = total + jnp.where(d < owner, counts[node, loader, d], 0)
    return total


def take_start(counts, node, loader, owner, length):
    total = jnp.int32(0)
    for s in range(length):
        total = total + jnp.where(s < loader, counts[node, s, owner], 0)
    return total


def project_kernel(n_i, indices, splits, slots, ids, counts, normed, table, bias, *refs):
    weights, outs = refs[: len(indices)], refs[len(indices) :]
    total = None
    for (piece, weight, split) in zip(indices, weights, splits):
        depth = normed.shape[2]
        for part in range(split):
            at = ids[3 + piece] + part
            term = jnp.dot(
                normed[at],
                weight[part * depth : (part + 1) * depth, :],
                preferred_element_type=jnp.float32,
            )
            total = term if total is None else total + term
    tile = rotate(total + bias[...], table[0, 0], table[0, 1]).astype(jnp.bfloat16)
    if not slots:
        outs[0][...] = tile
        return
    node, me = ids[0], ids[1]
    slot_rows, rows = outs[0].shape[0], tile.shape[0]
    source = lax.broadcasted_iota(jnp.int32, (slot_rows, rows), 1) - lax.broadcasted_iota(
        jnp.int32, (slot_rows, rows), 0
    )
    for shift, out in enumerate(outs):
        owner = lax.rem(me + shift, n_i)
        start = send_start(counts, node, me, owner, n_i)
        pick = jnp.where(source == start, 1.0, 0.0).astype(jnp.bfloat16)
        out[...] = jnp.dot(pick, tile, preferred_element_type=jnp.float32).astype(jnp.bfloat16)


def project(ids, counts, normed, table, bias, pieces, first_column, width, slot_rows, n_i):
    rows = normed.shape[1]
    depth = normed.shape[2]
    base = first_column // TILE
    weights = [p[0] for p in pieces]
    splits = tuple(w.shape[0] // depth for w in weights)
    offsets = [base if p[1] else 0 for p in pieces]
    slots = slot_rows is not None
    if slots:
        out_shape = [jax.ShapeDtypeStruct((slot_rows, width), jnp.bfloat16)] * n_i
        out_specs = [pl.BlockSpec((slot_rows, TILE), lambda c: (0, c))] * n_i
        table_spec = pl.BlockSpec((1, 2, rows, HEAD_SIZE), lambda c: (0, 0, 0, 0))
    else:
        out_shape = [jax.ShapeDtypeStruct((rows, width), jnp.bfloat16)]
        out_specs = [pl.BlockSpec((rows, TILE), lambda c: (0, c))]
        table_spec = pl.BlockSpec((1, 2, rows, HEAD_SIZE), lambda c: (c, 0, 0, 0))
    features = normed.shape[0] * depth
    return pl.pallas_call(
        functools.partial(project_kernel, n_i, tuple(range(len(pieces))), splits, slots),
        grid=(width // TILE,),
        in_specs=[
            smem(),
            smem(),
            whole_block(normed.shape),
            table_spec,
            pl.BlockSpec((1, TILE), lambda c: (0, base + c)),
        ]
        + [
            pl.BlockSpec((w.shape[0], TILE), functools.partial(lambda off, c: (0, off + c), off))
            for w, off in zip(weights, offsets)
        ],
        out_specs=out_specs,
        out_shape=out_shape,
        compiler_params=pltpu.CompilerParams(vmem_limit_bytes=VMEM_LIMIT),
        cost_estimate=pl.CostEstimate(
            flops=2 * rows * features * width,
            bytes_accessed=2 * features * (rows + width),
            transcendentals=0,
        ),
    )(ids, counts, normed, table, bias, *weights)


def reorder_kernel(n_i, ids, counts, *refs):
    arrived, out = refs[: 2 * n_i], refs[2 * n_i]
    block = pl.program_id(0)
    node, me, first = ids[0], ids[1], ids[2]
    rows = out.shape[0]

    @pl.when((block >= first // rows) & (block <= n_i + me))
    def _():
        place = lax.broadcasted_iota(jnp.int32, (rows, rows), 0)
        gap = lax.broadcasted_iota(jnp.int32, (rows, rows), 1) - place

        def gather(behind):
            owner = block - (0 if behind else n_i)
            which = jnp.maximum(node - 1, 0) if behind else node
            total = None
            for shift in range(n_i):
                loader = lax.rem(me + n_i - shift, n_i)
                start = take_start(counts, which, loader, owner, n_i)
                end = start + counts[which, loader, owner]
                source = send_start(counts, which, loader, owner, n_i)
                hit = (gap == source - start) & (place >= start) & (place < end)
                pick = jnp.where(hit, 1.0, 0.0).astype(jnp.bfloat16)
                held = arrived[(n_i if behind else 0) + shift][...]
                term = jnp.dot(pick, held, preferred_element_type=jnp.float32)
                total = term if total is None else total + term
            out[...] = total.astype(jnp.bfloat16)

        @pl.when(block < n_i)
        def _():
            gather(True)

        @pl.when(block >= n_i)
        def _():
            gather(False)


def reorder(ids, counts, arrived, n_i):
    rows, width = arrived[0].shape
    return pl.pallas_call(
        functools.partial(reorder_kernel, n_i),
        grid=(2 * n_i,),
        in_specs=[smem(), smem()] + [whole_block((rows, width))] * (2 * n_i),
        out_specs=pl.BlockSpec((rows, width), lambda b: (b, 0)),
        out_shape=jax.ShapeDtypeStruct((2 * n_i * rows, width), jnp.bfloat16),
        compiler_params=pltpu.CompilerParams(vmem_limit_bytes=VMEM_LIMIT),
        cost_estimate=pl.CostEstimate(
            flops=2 * (n_i + 1) * n_i * rows * rows * width,
            bytes_accessed=8 * n_i * rows * width,
            transcendentals=0,
        ),
    )(ids, counts, *arrived)


def attend_kernel(n_i, first_head, ids, counts, starts, key_values, *refs):
    slots, out, picks = refs[:n_i], refs[-2], refs[-1]
    node, me, first = ids[0], ids[1], ids[2]
    rows = out.shape[0]
    slot_rows = slots[0].shape[0]
    head = pl.program_id(0) + first_head

    @pl.when(pl.program_id(0) == 0)
    def _():
        place = lax.broadcasted_iota(jnp.int32, (rows, slot_rows), 0)
        inside = lax.broadcasted_iota(jnp.int32, (rows, slot_rows), 1)
        for shift in range(n_i):
            loader = lax.rem(me + n_i - shift, n_i)
            start = take_start(counts, node, loader, me, n_i)
            count = counts[node, loader, me]
            hit = (place - inside == start) & (inside < count)
            picks[shift] = jnp.where(hit, 1.0, 0.0).astype(jnp.bfloat16)

    queries = None
    for shift in range(n_i):
        term = jnp.dot(picks[shift], slots[shift][...], preferred_element_type=jnp.float32)
        queries = term if queries is None else queries + term
    queries = queries.astype(jnp.bfloat16)

    factor = math.log2(math.e) / math.sqrt(HEAD_SIZE)
    cut = rows // 3
    own = (n_i + me) * rows
    offset = lax.broadcasted_iota(jnp.int32, (cut, rows), 1)
    row = lax.broadcasted_iota(jnp.int32, (cut, rows), 0)
    group = head // QUERY_PER_KEY
    key_at = pl.ds(pl.multiple_of(group * HEAD_SIZE, HEAD_SIZE), HEAD_SIZE)
    value_at = pl.ds(pl.multiple_of(WIDTH_K + group * HEAD_SIZE, HEAD_SIZE), HEAD_SIZE)

    def step(block, carry):
        at = pl.ds(pl.multiple_of(block * rows, rows), rows)
        keys = key_values[at, key_at]
        values = key_values[at, value_at]
        after = []
        for part in range(3):
            highest, total, summed = carry[part]
            scores = lax.dot_general(
                queries[part * cut : (part + 1) * cut],
                keys,
                (((1,), (1,)), ((), ())),
                preferred_element_type=jnp.float32,
            )
            key = offset + block * rows
            seen = (key >= starts[part * cut : (part + 1) * cut, :]) & (
                key - row <= own + part * cut
            )
            scores = jnp.where(seen, scores * factor, MASKED)
            new = jnp.maximum(highest, jnp.max(scores, axis=1, keepdims=True))
            weights = jnp.exp2(scores - new)
            rescale = jnp.exp2(highest - new)
            total = total * rescale + jnp.sum(weights, axis=1, keepdims=True)
            summed = summed * rescale + jnp.dot(
                weights.astype(jnp.bfloat16), values, preferred_element_type=jnp.float32
            )
            after.append((new, total, summed))
        return tuple(after)

    fresh = (
        jnp.full((cut, 1), LEAST, jnp.float32),
        jnp.zeros((cut, 1), jnp.float32),
        jnp.zeros((cut, HEAD_SIZE), jnp.float32),
    )
    done = lax.fori_loop(first // rows, n_i + me + 1, step, (fresh,) * 3)
    for part, (_, total, summed) in enumerate(done):
        out[part * cut : (part + 1) * cut, :] = (summed / total).astype(jnp.bfloat16)


def attend(ids, counts, starts, key_values, slots, before, first_head, heads, n_i):
    rows = starts.shape[0]
    slot_rows = slots[0].shape[0]
    aliased = before is not None
    return pl.pallas_call(
        functools.partial(attend_kernel, n_i, first_head),
        grid=(heads,),
        in_specs=[smem(), smem(), whole_block(starts.shape), whole_block(key_values.shape)]
        + [pl.BlockSpec((slot_rows, HEAD_SIZE), lambda h: (0, h))] * n_i
        + ([pl.BlockSpec(memory_space=pl.ANY)] if aliased else []),
        out_specs=pl.BlockSpec((rows, HEAD_SIZE), lambda h: (0, first_head + h)),
        out_shape=jax.ShapeDtypeStruct((rows, WIDTH_Q), jnp.bfloat16),
        scratch_shapes=[pltpu.VMEM((n_i, rows, slot_rows), jnp.bfloat16)],
        input_output_aliases={4 + n_i: 0} if aliased else {},
        compiler_params=pltpu.CompilerParams(vmem_limit_bytes=VMEM_LIMIT),
        cost_estimate=pl.CostEstimate(
            flops=16 * heads * rows * rows * HEAD_SIZE,
            bytes_accessed=key_values.size * 2,
            transcendentals=4 * heads * rows * rows,
        ),
    )(ids, counts, starts, key_values, *slots, *([before] if aliased else []))


def on_device(hidden, gain, w_qkv, bias, boundaries, loader_counts):
    rows = hidden.shape[0]
    n_g, n_o, n_i = (lax.axis_size(a) for a in ("groups", "outer", "inner"))
    group, node, me = (lax.axis_index(a) for a in ("groups", "outer", "inner"))
    depth = w_qkv.shape[0] // n_g
    slot_rows = rows // n_i + rows // n_i // 2
    slot_rows = (slot_rows + 15) // 16 * 16

    columns = [(WIDTH_Q, 2 * WIDTH_K)]
    at = 0
    for heads in CHUNKS:
        columns.append((at * HEAD_SIZE, heads * HEAD_SIZE))
        at += heads
    beside = swapped(w_qkv, "outer")
    origins = [node * n_g, (node ^ 1) * n_g]
    chunk_pieces = []
    previous = None
    for first_column, width in columns:
        mine = lax.dynamic_slice(w_qkv, (group * depth, first_column), (depth, width))
        if previous is not None:
            mine, _ = lax.optimization_barrier((mine, previous))
        pieces = [(w_qkv, True), (beside, True)]
        where = list(origins)
        for hop in range(1, n_o // 2):
            across = shifted(mine, "outer", 2 * hop)
            previous = across
            source = lax.rem(node + n_o - 2 * hop, n_o)
            got = [(across, group)]
            for turn in range(1, n_g):
                got.append((shifted(across, "groups", turn), lax.rem(group + n_g - turn, n_g)))
            for array, part in got:
                pieces.append((array, False))
                where.append(source * n_g + part)
                pieces.append((swapped(array, "outer"), False))
                where.append((source ^ 1) * n_g + part)
        chunk_pieces.append(pieces)

    normed = normalize(hidden, gain, n_o * n_g)

    counts = lax.dynamic_index_in_dim(loader_counts, node, 0, keepdims=False)
    inside = jnp.arange(rows, dtype=jnp.int32)
    spans = jnp.arange(n_i, dtype=jnp.int32)
    before = spans[:, None] < spans[None, :]
    mine_counts = lax.dynamic_index_in_dim(counts, me, 0, keepdims=False)
    sends = jnp.sum(jnp.where(before, mine_counts[:, None], 0), axis=0)
    takes = jnp.sum(jnp.where((spans < me)[:, None], counts, 0), axis=0)
    reached = (sends[None, :] + mine_counts[None, :]) <= inside[:, None]
    owner = jnp.sum(reached.astype(jnp.int32), axis=1)
    jump = jnp.sum(
        jnp.where(owner[:, None] == spans[None, :], (takes - sends + spans * rows)[None, :], 0), axis=1
    )
    packed = node * n_i * rows + inside + jump
    position = packed - doc_starts(boundaries, packed)
    half = HEAD_SIZE // 2
    frequency = ROPE_BASE ** (-(jnp.arange(half, dtype=jnp.float32) * 2.0 / HEAD_SIZE))
    angles = position.astype(jnp.float32)[:, None] * frequency[None, :]
    cosine, sine = jnp.cos(angles), jnp.sin(angles)
    turned = jnp.stack(
        [jnp.concatenate([cosine, cosine], axis=1), jnp.concatenate([-sine, sine], axis=1)]
    )
    table = jnp.stack([turned, jnp.stack([jnp.ones_like(turned[0]), jnp.zeros_like(turned[0])])])

    base = (node - 1) * n_i * rows
    starts = doc_starts(boundaries, (node * n_i + me) * rows + inside) - base
    ids = jnp.stack([node, me, starts[0]] + where).astype(jnp.int32)
    starts = starts[:, None]
    bias = bias[None]

    def projected(chunk, slots):
        first_column, width = columns[chunk]
        return project(
            ids, loader_counts, normed, table, bias, chunk_pieces[chunk], first_column, width, slots, n_i
        )

    [key_values] = projected(0, None)
    held = [key_values] + [shifted(key_values, "inner", s) for s in range(1, n_i)]
    behind = [from_behind(array, "outer") for array in held]
    window = reorder(ids, loader_counts, held + behind, n_i)

    output = None
    at = 0
    for chunk, heads in enumerate(CHUNKS):
        slots = projected(1 + chunk, slot_rows)
        slots = [slots[0]] + [shifted(slots[s], "inner", s) for s in range(1, n_i)]
        output = attend(ids, loader_counts, starts, window, slots, output, at, heads, n_i)
        at += heads
    return output


def solution(mesh):
    in_specs = (
        P(("groups", "outer", "inner"), None),
        P(),
        P("outer", None),
        P(),
        P("groups"),
        P("groups", None, None),
    )
    out_specs = P(("groups", "outer", "inner"), None)
    return jax.shard_map(
        on_device, mesh=mesh, in_specs=in_specs, out_specs=out_specs, check_vma=False
    )
```

```python
import functools
import math

import jax
import jax.numpy as jnp
from jax import lax
from jax.experimental import pallas as pl
from jax.experimental.pallas import tpu as pltpu
from jax.sharding import PartitionSpec as P

HEAD_SIZE = 128
HQ = 14
KEY_VALUE_HEADS = 2
QUERY_PER_KEY = 7
DOC_MOST = 1536
EPSILON = 1e-06
ROPE_BASE = 1000000.0
LEAST = -1e30
MASKED = -2e30
WIDTH_Q = HQ * HEAD_SIZE
WIDTH_K = KEY_VALUE_HEADS * HEAD_SIZE
TILE = 2 * HEAD_SIZE
CHUNKS = (8, 6)
TOGETHER = (4, 2)
SHARED = (False, True, True)
VMEM_LIMIT = 40 * 1024 * 1024


def shifted(array, axis, by):
    length = lax.axis_size(axis)
    return lax.ppermute(array, axis, [(i, (i + by) % length) for i in range(length)])


def swapped(array, axis):
    length = lax.axis_size(axis)
    return lax.ppermute(array, axis, [(i, i ^ 1) for i in range(length)])


def from_behind(array, axis):
    length = lax.axis_size(axis)
    return lax.ppermute(array, axis, [(i, i + 1) for i in range(length - 1)])


def after(value, *others):
    return lax.optimization_barrier((value, others))[0]


def doc_starts(boundaries, token_positions):
    doc_ends = boundaries[1:]
    lengths = doc_ends - boundaries[:-1]
    passed = doc_ends[None, :] <= token_positions[:, None]
    return jnp.sum(jnp.where(passed, lengths[None, :], 0), axis=1)


def smem():
    return pl.BlockSpec(memory_space=pltpu.SMEM)


def whole_block(shape):
    return pl.BlockSpec(shape, lambda *_: (0,) * len(shape))


def norm_kernel(x_ref, gain_ref, out_ref):
    x = x_ref[...].astype(jnp.float32)
    scale = lax.rsqrt(jnp.mean(x * x, axis=1, keepdims=True) + EPSILON)
    y = (x * scale * gain_ref[...]).astype(jnp.bfloat16)
    depth = out_ref.shape[2]
    for k in range(out_ref.shape[0]):
        out_ref[k] = y[:, k * depth : (k + 1) * depth]


def normalize(hidden, gain, pieces):
    rows, features = hidden.shape
    step = rows // 3
    return pl.pallas_call(
        norm_kernel,
        grid=(rows // step,),
        in_specs=[
            pl.BlockSpec((step, features), lambda r: (r, 0)),
            whole_block((1, features)),
        ],
        out_specs=pl.BlockSpec((pieces, step, features // pieces), lambda r: (0, r, 0)),
        out_shape=jax.ShapeDtypeStruct((pieces, rows, features // pieces), jnp.bfloat16),
        compiler_params=pltpu.CompilerParams(vmem_limit_bytes=VMEM_LIMIT),
        cost_estimate=pl.CostEstimate(
            flops=4 * rows * features, bytes_accessed=4 * rows * features, transcendentals=rows
        ),
    )(hidden, gain[None])


def rotate(tile, cosine, sine):
    parts = []
    for h in range(tile.shape[1] // HEAD_SIZE):
        x = tile[:, h * HEAD_SIZE : (h + 1) * HEAD_SIZE]
        parts.append(x * cosine + pltpu.roll(x, HEAD_SIZE // 2, 1) * sine)
    return jnp.concatenate(parts, axis=1)


def send_start(counts, node, loader, owner, length):
    total = jnp.int32(0)
    for d in range(length):
        total = total + jnp.where(d < owner, counts[node, loader, d], 0)
    return total


def take_start(counts, node, loader, owner, length):
    total = jnp.int32(0)
    for s in range(length):
        total = total + jnp.where(s < loader, counts[node, s, owner], 0)
    return total


def project_kernel(n_i, indices, splits, slots, ids, counts, normed, table, bias, *refs):
    weights, outs = refs[: len(indices)], refs[len(indices) :]
    total = None
    for (piece, weight, split) in zip(indices, weights, splits):
        depth = normed.shape[2]
        for part in range(split):
            at = ids[3 + piece] + part
            term = jnp.dot(
                normed[at],
                weight[part * depth : (part + 1) * depth, :],
                preferred_element_type=jnp.float32,
            )
            total = term if total is None else total + term
    tile = rotate(total + bias[...], table[0, 0], table[0, 1]).astype(jnp.bfloat16)
    if not slots:
        outs[0][...] = tile
        return
    node, me = ids[0], ids[1]
    slot_rows, rows = outs[0].shape[0], tile.shape[0]
    source = lax.broadcasted_iota(jnp.int32, (slot_rows, rows), 1) - lax.broadcasted_iota(
        jnp.int32, (slot_rows, rows), 0
    )
    for shift, out in enumerate(outs):
        owner = lax.rem(me + shift, n_i)
        start = send_start(counts, node, me, owner, n_i)
        pick = jnp.where(source == start, 1.0, 0.0).astype(jnp.bfloat16)
        out[...] = jnp.dot(pick, tile, preferred_element_type=jnp.float32).astype(jnp.bfloat16)


def project(ids, counts, normed, table, bias, pieces, first_column, width, slot_rows, n_i):
    rows = normed.shape[1]
    depth = normed.shape[2]
    base = first_column // TILE
    weights = [p[0] for p in pieces]
    splits = tuple(w.shape[0] // depth for w in weights)
    offsets = [base if p[1] < 2 else 0 for p in pieces]
    slots = slot_rows is not None
    if slots:
        out_shape = [jax.ShapeDtypeStruct((slot_rows, width), jnp.bfloat16)] * n_i
        out_specs = [pl.BlockSpec((slot_rows, TILE), lambda c: (0, c))] * n_i
        table_spec = pl.BlockSpec((1, 2, rows, HEAD_SIZE), lambda c: (0, 0, 0, 0))
    else:
        out_shape = [jax.ShapeDtypeStruct((rows, width), jnp.bfloat16)]
        out_specs = [pl.BlockSpec((rows, TILE), lambda c: (0, c))]
        table_spec = pl.BlockSpec((1, 2, rows, HEAD_SIZE), lambda c: (c, 0, 0, 0))
    features = normed.shape[0] * depth
    return pl.pallas_call(
        functools.partial(project_kernel, n_i, tuple(p[1] for p in pieces), splits, slots),
        grid=(width // TILE,),
        in_specs=[
            smem(),
            smem(),
            whole_block(normed.shape),
            table_spec,
            pl.BlockSpec((1, TILE), lambda c: (0, base + c)),
        ]
        + [
            pl.BlockSpec((w.shape[0], TILE), functools.partial(lambda off, c: (0, off + c), off))
            for w, off in zip(weights, offsets)
        ],
        out_specs=out_specs,
        out_shape=out_shape,
        compiler_params=pltpu.CompilerParams(vmem_limit_bytes=VMEM_LIMIT),
        cost_estimate=pl.CostEstimate(
            flops=2 * rows * features * width,
            bytes_accessed=2 * features * (rows + width),
            transcendentals=0,
        ),
    )(ids, counts, normed, table, bias, *weights)


def reorder_kernel(n_i, reach, ids, counts, held, behind, keys_out, values_out):
    block = pl.program_id(0)
    node, me, first = ids[0], ids[1], ids[2]
    rows = held.shape[1]

    @pl.when((block >= first // rows) & (block <= n_i + me))
    def _():
        place = lax.broadcasted_iota(jnp.int32, (rows, reach), 0)
        gap = lax.broadcasted_iota(jnp.int32, (rows, reach), 1) - place

        def gather(arrived, which, owner):
            total = None
            for shift in range(n_i):
                loader = lax.rem(me + n_i - shift, n_i)
                start = take_start(counts, which, loader, owner, n_i)
                end = start + counts[which, loader, owner]
                source = send_start(counts, which, loader, owner, n_i)
                at = pl.multiple_of(jnp.minimum(source // 16 * 16, rows - reach), 16)
                hit = (gap == source - start - at) & (place >= start) & (place < end)
                pick = jnp.where(hit, 1.0, 0.0).astype(jnp.bfloat16)
                term = jnp.dot(
                    pick, arrived[shift, pl.ds(at, reach), :], preferred_element_type=jnp.float32
                )
                total = term if total is None else total + term
            keys_out[0] = total[:, :WIDTH_K].T.astype(jnp.bfloat16)
            values_out[0] = total[:, WIDTH_K:].astype(jnp.bfloat16)

        @pl.when(block < n_i)
        def _():
            gather(behind, jnp.maximum(node - 1, 0), block)

        @pl.when(block >= n_i)
        def _():
            gather(held, node, block - n_i)


def reorder(ids, counts, held, behind, reach):
    n_i, rows, width = held.shape
    return pl.pallas_call(
        functools.partial(reorder_kernel, n_i, reach),
        grid=(2 * n_i,),
        in_specs=[smem(), smem(), whole_block(held.shape), whole_block(held.shape)],
        out_specs=[
            pl.BlockSpec((1, WIDTH_K, rows), lambda b: (b, 0, 0)),
            pl.BlockSpec((1, rows, WIDTH_K), lambda b: (b, 0, 0)),
        ],
        out_shape=[
            jax.ShapeDtypeStruct((2 * n_i, WIDTH_K, rows), jnp.bfloat16),
            jax.ShapeDtypeStruct((2 * n_i, rows, WIDTH_K), jnp.bfloat16),
        ],
        compiler_params=pltpu.CompilerParams(vmem_limit_bytes=VMEM_LIMIT),
        cost_estimate=pl.CostEstimate(
            flops=2 * (n_i + 1) * n_i * rows * rows * width,
            bytes_accessed=8 * n_i * rows * width,
            transcendentals=0,
        ),
    )(ids, counts, held, behind)


def attend_kernel(n_i, first_head, heads, pair, ids, counts, starts, keys, values, *refs):
    slots, refs = refs[:n_i], refs[-8:]
    out, queries, bias, scores, peak, highest, total, summed = refs
    node, me, first = ids[0], ids[1], ids[2]
    rows = out.shape[0]
    slot_rows = slots[0].shape[0]
    at = pl.program_id(0)
    low, high = first // rows, n_i + me + 1
    factor = math.log2(math.e) / math.sqrt(HEAD_SIZE)

    @pl.when(at == 0)
    def _():
        place = lax.broadcasted_iota(jnp.int32, (rows, slot_rows), 0)
        inside = lax.broadcasted_iota(jnp.int32, (rows, slot_rows), 1)
        gathered = None
        for shift in range(n_i):
            loader = lax.rem(me + n_i - shift, n_i)
            start = take_start(counts, node, loader, me, n_i)
            hit = (place - inside == start) & (inside < counts[node, loader, me])
            pick = jnp.where(hit, 1.0, 0.0).astype(jnp.bfloat16)
            term = jnp.dot(pick, slots[shift][...], preferred_element_type=jnp.float32)
            gathered = term if gathered is None else gathered + term
        queries[...] = gathered.astype(jnp.bfloat16)
        ahead = lax.broadcasted_iota(jnp.int32, (rows, rows), 1)
        row = lax.broadcasted_iota(jnp.int32, (rows, rows), 0)

        def shade(block, carry):
            seen = (ahead >= starts[...] - block * rows) & (
                ahead - row <= (n_i + me - block) * rows
            )
            bias[block - low] = jnp.where(seen, 0.0, MASKED)
            return carry

        lax.fori_loop(low, high, shade, 0)

    def lanes(index):
        return pl.ds(pl.multiple_of(index * HEAD_SIZE, HEAD_SIZE), HEAD_SIZE)

    def run(form, weigh):
        now, then = lax.rem(at, 2), lax.rem(at + 1, 2)
        if form:
            peak[now] = jnp.full(peak.shape[1:], LEAST, jnp.float32)
        if weigh:
            top = jnp.max(peak[then], axis=2, keepdims=True) * factor
            highest[...] = jnp.broadcast_to(top, highest.shape)
            total[...] = jnp.zeros(total.shape, jnp.float32)
            summed[...] = jnp.zeros(summed.shape, jnp.float32)

        def step(block, carry):
            for j in range(pair):
                if form:
                    head = at * pair + j
                    key = keys[block, lanes((first_head + head) // QUERY_PER_KEY), :]
                    score = jnp.dot(
                        queries[:, lanes(head)], key, preferred_element_type=jnp.float32
                    )
                    score = score + bias[block - low]
                    scores[now, j, block - low] = score
                    best = peak[now, j]
                    for k in range(rows // HEAD_SIZE):
                        best = jnp.maximum(best, score[:, k * HEAD_SIZE : (k + 1) * HEAD_SIZE])
                    peak[now, j] = best
                if weigh:
                    head = (at - 1) * pair + j
                    value = values[block, :, lanes((first_head + head) // QUERY_PER_KEY)]
                    weights = []
                    add = total[j]
                    for k in range(rows // HEAD_SIZE):
                        score = scores[then, j, block - low, :, k * HEAD_SIZE : (k + 1) * HEAD_SIZE]
                        weight = jnp.exp2(score * factor - highest[j])
                        add = add + weight
                        weights.append(weight.astype(jnp.bfloat16))
                    total[j] = add
                    summed[j] += jnp.dot(
                        jnp.concatenate(weights, axis=1), value, preferred_element_type=jnp.float32
                    )
            return carry

        lax.fori_loop(low, high, step, 0)
        if weigh:
            for j in range(pair):
                whole = jnp.sum(total[j], axis=1, keepdims=True)
                out[:, j * HEAD_SIZE : (j + 1) * HEAD_SIZE] = (summed[j] / whole).astype(
                    jnp.bfloat16
                )

    @pl.when(at == 0)
    def _():
        run(True, False)

    @pl.when((at > 0) & (at < heads // pair))
    def _():
        run(True, True)

    @pl.when(at == heads // pair)
    def _():
        run(False, True)


def attend(ids, counts, starts, keys, values, slots, before, first_head, heads, pair):
    rows = starts.shape[0]
    n_i = len(slots)
    slot_rows, width = slots[0].shape
    aliased = before is not None
    wide = (rows, HEAD_SIZE)
    blocks = (DOC_MOST + rows - 2) // rows + 1
    return pl.pallas_call(
        functools.partial(attend_kernel, n_i, first_head, heads, pair),
        grid=(heads // pair + 1,),
        in_specs=[
            smem(),
            smem(),
            whole_block(starts.shape),
            whole_block(keys.shape),
            whole_block(values.shape),
        ]
        + [whole_block((slot_rows, width))] * n_i
        + ([pl.BlockSpec(memory_space=pl.ANY)] if aliased else []),
        out_specs=pl.BlockSpec(
            (rows, pair * HEAD_SIZE), lambda h: (0, first_head // pair + jnp.maximum(h - 1, 0))
        ),
        out_shape=jax.ShapeDtypeStruct((rows, WIDTH_Q), jnp.bfloat16),
        scratch_shapes=[
            pltpu.VMEM((rows, width), jnp.bfloat16),
            pltpu.VMEM((blocks, rows, rows), jnp.float32),
            pltpu.VMEM((2, pair, blocks, rows, rows), jnp.float32),
            pltpu.VMEM((2, pair, *wide), jnp.float32),
            pltpu.VMEM((pair, *wide), jnp.float32),
            pltpu.VMEM((pair, *wide), jnp.float32),
            pltpu.VMEM((pair, *wide), jnp.float32),
        ],
        input_output_aliases={5 + n_i: 0} if aliased else {},
        compiler_params=pltpu.CompilerParams(vmem_limit_bytes=VMEM_LIMIT),
        cost_estimate=pl.CostEstimate(
            flops=16 * heads * rows * rows * HEAD_SIZE,
            bytes_accessed=keys.size * 4,
            transcendentals=4 * heads * rows * rows,
        ),
    )(ids, counts, starts, keys, values, *slots, *([before] if aliased else []))


def on_device(hidden, gain, w_qkv, bias, boundaries, loader_counts):
    rows = hidden.shape[0]
    n_g, n_o, n_i = (lax.axis_size(a) for a in ("groups", "outer", "inner"))
    group, node, me = (lax.axis_index(a) for a in ("groups", "outer", "inner"))
    depth = w_qkv.shape[0] // n_g
    slot_rows = rows // n_i + rows // n_i // 2
    slot_rows = (slot_rows + 15) // 16 * 16

    columns = [(WIDTH_Q, 2 * WIDTH_K)]
    at = 0
    for heads in CHUNKS:
        columns.append((at * HEAD_SIZE, heads * HEAD_SIZE))
        at += heads
    beside = swapped(w_qkv, "outer")
    hops = range(1, n_o // 2)
    sources = [lax.rem(node + n_o - 2 * hop, n_o) for hop in hops]
    parts = [lax.rem(group + n_g - turn, n_g) for turn in range(n_g)]
    where = [node * n_g, (node ^ 1) * n_g]
    for source in sources:
        where += [source * n_g, (source ^ 1) * n_g]
    shared_from = len(where)
    for source in sources:
        for part in parts:
            where += [source * n_g + part, (source ^ 1) * n_g + part]

    def cut(chunk):
        first_column, width = columns[chunk]
        if SHARED[chunk]:
            return lax.dynamic_slice(w_qkv, (group * depth, first_column), (depth, width))
        return w_qkv[:, first_column : first_column + width]

    def cross(array):
        return [shifted(array, "outer", 2 * hop) for hop in hops]

    def passed(chunk, arrived):
        turns = range(1, n_g if SHARED[chunk] else 1)
        return [[a] + [shifted(a, "groups", turn) for turn in turns] for a in arrived]

    def spread(chunk, arrived):
        pieces = [(w_qkv, 0), (beside, 1)]
        at = shared_from if SHARED[chunk] else 2
        for got in arrived:
            for array in got:
                pieces += [(array, at), (swapped(array, "outer"), at + 1)]
                at += 2
        return pieces

    def around(first, others):
        return [first] + [shifted(array, "inner", 1 + s) for s, array in enumerate(others)]

    normed = normalize(hidden, gain, n_o * n_g)

    counts = lax.dynamic_index_in_dim(loader_counts, node, 0, keepdims=False)
    inside = jnp.arange(rows, dtype=jnp.int32)
    spans = jnp.arange(n_i, dtype=jnp.int32)
    before = spans[:, None] < spans[None, :]
    mine_counts = lax.dynamic_index_in_dim(counts, me, 0, keepdims=False)
    sends = jnp.sum(jnp.where(before, mine_counts[:, None], 0), axis=0)
    takes = jnp.sum(jnp.where((spans < me)[:, None], counts, 0), axis=0)
    reached = (sends[None, :] + mine_counts[None, :]) <= inside[:, None]
    owner = jnp.sum(reached.astype(jnp.int32), axis=1)
    jump = jnp.sum(
        jnp.where(owner[:, None] == spans[None, :], (takes - sends + spans * rows)[None, :], 0), axis=1
    )
    packed = node * n_i * rows + inside + jump
    position = packed - doc_starts(boundaries, packed)
    half = HEAD_SIZE // 2
    frequency = ROPE_BASE ** (-(jnp.arange(half, dtype=jnp.float32) * 2.0 / HEAD_SIZE))
    angles = position.astype(jnp.float32)[:, None] * frequency[None, :]
    cosine, sine = jnp.cos(angles), jnp.sin(angles)
    turned = jnp.stack(
        [jnp.concatenate([cosine, cosine], axis=1), jnp.concatenate([-sine, sine], axis=1)]
    )
    table = jnp.stack([turned, jnp.stack([jnp.ones_like(turned[0]), jnp.zeros_like(turned[0])])])

    base = (node - 1) * n_i * rows
    starts = doc_starts(boundaries, (node * n_i + me) * rows + inside) - base
    ids = jnp.stack([node, me, starts[0]] + where).astype(jnp.int32)
    starts = starts[:, None]
    bias = bias[None]

    def projected(chunk, pieces, slots):
        first_column, width = columns[chunk]
        return project(
            ids, loader_counts, normed, table, bias, pieces, first_column, width, slots, n_i
        )

    arrived, normed, table, ids, starts, waiting = lax.optimization_barrier(
        (
            cross(cut(0)),
            normed,
            table,
            ids,
            starts,
            [cut(chunk) for chunk in range(1, len(columns))],
        )
    )
    crossing = cross(waiting[0])
    [key_values] = projected(0, spread(0, passed(0, arrived)), None)
    held = around(key_values, [key_values] * (n_i - 1))
    stacked = jnp.stack(held)
    behind = from_behind(stacked, "outer")

    crossing, waiting, _ = lax.optimization_barrier((crossing, waiting, held[1]))
    first, crossing = lax.optimization_barrier((passed(1, crossing), cross(waiting[1])))
    outs = projected(1, spread(1, after(first, stacked)), slot_rows)
    slots = [around(outs[0], outs[1:])]
    second = passed(2, crossing)
    keys, values = reorder(
        ids, loader_counts, after(stacked, outs[0], second), behind, slot_rows + 16
    )
    outs = projected(2, spread(2, after(second, slots[0], keys)), slot_rows)
    slots.append(around(outs[0], outs[1:]))

    output = None
    at = 0
    for chunk, heads in enumerate(CHUNKS):
        output = attend(
            ids, loader_counts, starts, keys, values, slots[chunk], output, at, heads, TOGETHER[chunk]
        )
        at += heads
    return output


def solution(mesh):
    in_specs = (
        P(("groups", "outer", "inner"), None),
        P(),
        P("outer", None),
        P(),
        P("groups"),
        P("groups", None, None),
    )
    out_specs = P(("groups", "outer", "inner"), None)
    return jax.shard_map(
        on_device, mesh=mesh, in_specs=in_specs, out_specs=out_specs, check_vma=False
    )
```

```python
import functools
import math

import jax
import jax.numpy as jnp
from jax import lax
from jax.experimental import pallas as pl
from jax.experimental.pallas import tpu as pltpu
from jax.sharding import PartitionSpec as P

HEAD_SIZE = 128
HQ = 14
KEY_VALUE_HEADS = 2
QUERY_PER_KEY = 7
DOC_MOST = 1536
EPSILON = 1e-06
ROPE_BASE = 1000000.0
LEAST = -1e30
MASKED = -2e30
WIDTH_Q = HQ * HEAD_SIZE
WIDTH_K = KEY_VALUE_HEADS * HEAD_SIZE
TILE = 2 * HEAD_SIZE
CHUNKS = (8, 6)
TOGETHER = (4, 2)
SHARED = (False, False, True, True)
VMEM_LIMIT = 40 * 1024 * 1024


def shifted(array, axis, by):
    length = lax.axis_size(axis)
    return lax.ppermute(array, axis, [(i, (i + by) % length) for i in range(length)])


def swapped(array, axis):
    length = lax.axis_size(axis)
    return lax.ppermute(array, axis, [(i, i ^ 1) for i in range(length)])


def from_behind(array, axis):
    length = lax.axis_size(axis)
    return lax.ppermute(array, axis, [(i, i + 1) for i in range(length - 1)])


def after(value, *others):
    return lax.optimization_barrier((value, others))[0]


def doc_starts(boundaries, token_positions):
    doc_ends = boundaries[1:]
    lengths = doc_ends - boundaries[:-1]
    passed = doc_ends[None, :] <= token_positions[:, None]
    return jnp.sum(jnp.where(passed, lengths[None, :], 0), axis=1)


def smem():
    return pl.BlockSpec(memory_space=pltpu.SMEM)


def whole_block(shape):
    return pl.BlockSpec(shape, lambda *_: (0,) * len(shape))


def norm_kernel(x_ref, gain_ref, out_ref):
    x = x_ref[...].astype(jnp.float32)
    scale = lax.rsqrt(jnp.mean(x * x, axis=1, keepdims=True) + EPSILON)
    y = (x * scale * gain_ref[...]).astype(jnp.bfloat16)
    depth = out_ref.shape[2]
    for k in range(out_ref.shape[0]):
        out_ref[k] = y[:, k * depth : (k + 1) * depth]


def normalize(hidden, gain, pieces):
    rows, features = hidden.shape
    step = rows // 3
    return pl.pallas_call(
        norm_kernel,
        grid=(rows // step,),
        in_specs=[
            pl.BlockSpec((step, features), lambda r: (r, 0)),
            whole_block((1, features)),
        ],
        out_specs=pl.BlockSpec((pieces, step, features // pieces), lambda r: (0, r, 0)),
        out_shape=jax.ShapeDtypeStruct((pieces, rows, features // pieces), jnp.bfloat16),
        compiler_params=pltpu.CompilerParams(vmem_limit_bytes=VMEM_LIMIT),
        cost_estimate=pl.CostEstimate(
            flops=4 * rows * features, bytes_accessed=4 * rows * features, transcendentals=rows
        ),
    )(hidden, gain[None])


def rotate(tile, cosine, sine):
    parts = []
    for h in range(tile.shape[1] // HEAD_SIZE):
        x = tile[:, h * HEAD_SIZE : (h + 1) * HEAD_SIZE]
        parts.append(x * cosine + pltpu.roll(x, HEAD_SIZE // 2, 1) * sine)
    return jnp.concatenate(parts, axis=1)


def send_start(counts, node, loader, owner, length):
    total = jnp.int32(0)
    for d in range(length):
        total = total + jnp.where(d < owner, counts[node, loader, d], 0)
    return total


def take_start(counts, node, loader, owner, length):
    total = jnp.int32(0)
    for s in range(length):
        total = total + jnp.where(s < loader, counts[node, s, owner], 0)
    return total


def project_kernel(n_i, indices, splits, slots, ids, counts, normed, table, bias, *refs):
    weights, outs = refs[: len(indices)], refs[len(indices) :]
    total = None
    for (piece, weight, split) in zip(indices, weights, splits):
        depth = normed.shape[2]
        for part in range(split):
            at = ids[3 + piece] + part
            term = jnp.dot(
                normed[at],
                weight[part * depth : (part + 1) * depth, :],
                preferred_element_type=jnp.float32,
            )
            total = term if total is None else total + term
    tile = rotate(total + bias[...], table[0, 0], table[0, 1]).astype(jnp.bfloat16)
    if not slots:
        outs[0][...] = tile
        return
    node, me = ids[0], ids[1]
    slot_rows, rows = outs[0].shape[0], tile.shape[0]
    source = lax.broadcasted_iota(jnp.int32, (slot_rows, rows), 1) - lax.broadcasted_iota(
        jnp.int32, (slot_rows, rows), 0
    )
    for shift, out in enumerate(outs):
        owner = lax.rem(me + shift, n_i)
        start = send_start(counts, node, me, owner, n_i)
        pick = jnp.where(source == start, 1.0, 0.0).astype(jnp.bfloat16)
        out[...] = jnp.dot(pick, tile, preferred_element_type=jnp.float32).astype(jnp.bfloat16)


def project(ids, counts, normed, table, bias, pieces, first_column, width, slot_rows, n_i):
    rows = normed.shape[1]
    depth = normed.shape[2]
    base = first_column // TILE
    weights = [p[0] for p in pieces]
    splits = tuple(w.shape[0] // depth for w in weights)
    offsets = [base if p[1] < 2 else 0 for p in pieces]
    slots = slot_rows is not None
    if slots:
        out_shape = [jax.ShapeDtypeStruct((slot_rows, width), jnp.bfloat16)] * n_i
        out_specs = [pl.BlockSpec((slot_rows, TILE), lambda c: (0, c))] * n_i
        table_spec = pl.BlockSpec((1, 2, rows, HEAD_SIZE), lambda c: (0, 0, 0, 0))
    else:
        out_shape = [jax.ShapeDtypeStruct((rows, width), jnp.bfloat16)]
        out_specs = [pl.BlockSpec((rows, TILE), lambda c: (0, c))]
        still = first_column // (WIDTH_Q + WIDTH_K)
        table_spec = pl.BlockSpec((1, 2, rows, HEAD_SIZE), lambda c: (still, 0, 0, 0))
    features = normed.shape[0] * depth
    return pl.pallas_call(
        functools.partial(project_kernel, n_i, tuple(p[1] for p in pieces), splits, slots),
        grid=(width // TILE,),
        in_specs=[
            smem(),
            smem(),
            whole_block(normed.shape),
            table_spec,
            pl.BlockSpec((1, TILE), lambda c: (0, base + c)),
        ]
        + [
            pl.BlockSpec((w.shape[0], TILE), functools.partial(lambda off, c: (0, off + c), off))
            for w, off in zip(weights, offsets)
        ],
        out_specs=out_specs,
        out_shape=out_shape,
        compiler_params=pltpu.CompilerParams(vmem_limit_bytes=VMEM_LIMIT),
        cost_estimate=pl.CostEstimate(
            flops=2 * rows * features * width,
            bytes_accessed=2 * features * (rows + width),
            transcendentals=0,
        ),
    )(ids, counts, normed, table, bias, *weights)


def reorder_kernel(n_i, reach, ids, counts, held, behind, keys_out, values_out):
    block = pl.program_id(0)
    node, me, first = ids[0], ids[1], ids[2]
    rows = held.shape[1]

    @pl.when((block >= first // rows) & (block <= n_i + me))
    def _():
        place = lax.broadcasted_iota(jnp.int32, (rows, reach), 0)
        gap = lax.broadcasted_iota(jnp.int32, (rows, reach), 1) - place

        def gather(arrived, which, owner):
            total = None
            for shift in range(n_i):
                loader = lax.rem(me + n_i - shift, n_i)
                start = take_start(counts, which, loader, owner, n_i)
                end = start + counts[which, loader, owner]
                source = send_start(counts, which, loader, owner, n_i)
                at = pl.multiple_of(jnp.minimum(source // 16 * 16, rows - reach), 16)
                hit = (gap == source - start - at) & (place >= start) & (place < end)
                pick = jnp.where(hit, 1.0, 0.0).astype(jnp.bfloat16)
                term = jnp.dot(
                    pick, arrived[shift, pl.ds(at, reach), :], preferred_element_type=jnp.float32
                )
                total = term if total is None else total + term
            keys_out[0] = total[:, :WIDTH_K].T.astype(jnp.bfloat16)
            values_out[0] = total[:, WIDTH_K:].astype(jnp.bfloat16)

        @pl.when(block < n_i)
        def _():
            gather(behind, jnp.maximum(node - 1, 0), block)

        @pl.when(block >= n_i)
        def _():
            gather(held, node, block - n_i)


def reorder(ids, counts, held, behind, reach):
    n_i, rows, width = held.shape
    return pl.pallas_call(
        functools.partial(reorder_kernel, n_i, reach),
        grid=(2 * n_i,),
        in_specs=[smem(), smem(), whole_block(held.shape), whole_block(held.shape)],
        out_specs=[
            pl.BlockSpec((1, WIDTH_K, rows), lambda b: (b, 0, 0)),
            pl.BlockSpec((1, rows, WIDTH_K), lambda b: (b, 0, 0)),
        ],
        out_shape=[
            jax.ShapeDtypeStruct((2 * n_i, WIDTH_K, rows), jnp.bfloat16),
            jax.ShapeDtypeStruct((2 * n_i, rows, WIDTH_K), jnp.bfloat16),
        ],
        compiler_params=pltpu.CompilerParams(vmem_limit_bytes=VMEM_LIMIT),
        cost_estimate=pl.CostEstimate(
            flops=2 * (n_i + 1) * n_i * rows * rows * width,
            bytes_accessed=8 * n_i * rows * width,
            transcendentals=0,
        ),
    )(ids, counts, held, behind)


def attend_kernel(n_i, first_head, heads, pair, ids, counts, starts, keys, values, *refs):
    slots, refs = refs[:n_i], refs[-8:]
    out, queries, bias, scores, peak, highest, total, summed = refs
    node, me, first = ids[0], ids[1], ids[2]
    rows = out.shape[0]
    slot_rows = slots[0].shape[0]
    at = pl.program_id(0)
    low, high = first // rows, n_i + me + 1
    factor = math.log2(math.e) / math.sqrt(HEAD_SIZE)

    @pl.when(at == 0)
    def _():
        place = lax.broadcasted_iota(jnp.int32, (rows, slot_rows), 0)
        inside = lax.broadcasted_iota(jnp.int32, (rows, slot_rows), 1)
        gathered = None
        for shift in range(n_i):
            loader = lax.rem(me + n_i - shift, n_i)
            start = take_start(counts, node, loader, me, n_i)
            hit = (place - inside == start) & (inside < counts[node, loader, me])
            pick = jnp.where(hit, 1.0, 0.0).astype(jnp.bfloat16)
            term = jnp.dot(pick, slots[shift][...], preferred_element_type=jnp.float32)
            gathered = term if gathered is None else gathered + term
        queries[...] = gathered.astype(jnp.bfloat16)
        ahead = lax.broadcasted_iota(jnp.int32, (rows, rows), 1)
        row = lax.broadcasted_iota(jnp.int32, (rows, rows), 0)

        def shade(block, carry):
            seen = (ahead >= starts[...] - block * rows) & (
                ahead - row <= (n_i + me - block) * rows
            )
            bias[block - low] = jnp.where(seen, 0.0, MASKED)
            return carry

        lax.fori_loop(low, high, shade, 0)

    def lanes(index):
        return pl.ds(pl.multiple_of(index * HEAD_SIZE, HEAD_SIZE), HEAD_SIZE)

    def run(form, weigh):
        now, then = lax.rem(at, 2), lax.rem(at + 1, 2)
        if form:
            peak[now] = jnp.full(peak.shape[1:], LEAST, jnp.float32)
        if weigh:
            top = jnp.max(peak[then], axis=2, keepdims=True) * factor
            highest[...] = jnp.broadcast_to(top, highest.shape)
            total[...] = jnp.zeros(total.shape, jnp.float32)
            summed[...] = jnp.zeros(summed.shape, jnp.float32)

        def step(block, carry):
            for j in range(pair):
                if form:
                    head = at * pair + j
                    key = keys[block, lanes((first_head + head) // QUERY_PER_KEY), :]
                    score = jnp.dot(
                        queries[:, lanes(head)], key, preferred_element_type=jnp.float32
                    )
                    score = score + bias[block - low]
                    scores[now, j, block - low] = score
                    best = peak[now, j]
                    for k in range(rows // HEAD_SIZE):
                        best = jnp.maximum(best, score[:, k * HEAD_SIZE : (k + 1) * HEAD_SIZE])
                    peak[now, j] = best
                if weigh:
                    head = (at - 1) * pair + j
                    value = values[block, :, lanes((first_head + head) // QUERY_PER_KEY)]
                    weights = []
                    add = total[j]
                    for k in range(rows // HEAD_SIZE):
                        score = scores[then, j, block - low, :, k * HEAD_SIZE : (k + 1) * HEAD_SIZE]
                        weight = jnp.exp2(score * factor - highest[j])
                        add = add + weight
                        weights.append(weight.astype(jnp.bfloat16))
                    total[j] = add
                    summed[j] += jnp.dot(
                        jnp.concatenate(weights, axis=1), value, preferred_element_type=jnp.float32
                    )
            return carry

        lax.fori_loop(low, high, step, 0)
        if weigh:
            for j in range(pair):
                whole = jnp.sum(total[j], axis=1, keepdims=True)
                out[:, j * HEAD_SIZE : (j + 1) * HEAD_SIZE] = (summed[j] / whole).astype(
                    jnp.bfloat16
                )

    @pl.when(at == 0)
    def _():
        run(True, False)

    @pl.when((at > 0) & (at < heads // pair))
    def _():
        run(True, True)

    @pl.when(at == heads // pair)
    def _():
        run(False, True)


def attend(ids, counts, starts, keys, values, slots, before, first_head, heads, pair):
    rows = starts.shape[0]
    n_i = len(slots)
    slot_rows, width = slots[0].shape
    aliased = before is not None
    wide = (rows, HEAD_SIZE)
    blocks = (DOC_MOST + rows - 2) // rows + 1
    return pl.pallas_call(
        functools.partial(attend_kernel, n_i, first_head, heads, pair),
        grid=(heads // pair + 1,),
        in_specs=[
            smem(),
            smem(),
            whole_block(starts.shape),
            whole_block(keys.shape),
            whole_block(values.shape),
        ]
        + [whole_block((slot_rows, width))] * n_i
        + ([pl.BlockSpec(memory_space=pl.ANY)] if aliased else []),
        out_specs=pl.BlockSpec(
            (rows, pair * HEAD_SIZE), lambda h: (0, first_head // pair + jnp.maximum(h - 1, 0))
        ),
        out_shape=jax.ShapeDtypeStruct((rows, WIDTH_Q), jnp.bfloat16),
        scratch_shapes=[
            pltpu.VMEM((rows, width), jnp.bfloat16),
            pltpu.VMEM((blocks, rows, rows), jnp.float32),
            pltpu.VMEM((2, pair, blocks, rows, rows), jnp.float32),
            pltpu.VMEM((2, pair, *wide), jnp.float32),
            pltpu.VMEM((pair, *wide), jnp.float32),
            pltpu.VMEM((pair, *wide), jnp.float32),
            pltpu.VMEM((pair, *wide), jnp.float32),
        ],
        input_output_aliases={5 + n_i: 0} if aliased else {},
        compiler_params=pltpu.CompilerParams(vmem_limit_bytes=VMEM_LIMIT),
        cost_estimate=pl.CostEstimate(
            flops=16 * heads * rows * rows * HEAD_SIZE,
            bytes_accessed=keys.size * 4,
            transcendentals=4 * heads * rows * rows,
        ),
    )(ids, counts, starts, keys, values, *slots, *([before] if aliased else []))


def on_device(hidden, gain, w_qkv, bias, boundaries, loader_counts):
    rows = hidden.shape[0]
    n_g, n_o, n_i = (lax.axis_size(a) for a in ("groups", "outer", "inner"))
    group, node, me = (lax.axis_index(a) for a in ("groups", "outer", "inner"))
    depth = w_qkv.shape[0] // n_g
    slot_rows = rows // n_i + rows // n_i // 2
    slot_rows = (slot_rows + 15) // 16 * 16

    columns = [(WIDTH_Q, WIDTH_K), (WIDTH_Q + WIDTH_K, WIDTH_K)]
    at = 0
    for heads in CHUNKS:
        columns.append((at * HEAD_SIZE, heads * HEAD_SIZE))
        at += heads
    beside = swapped(w_qkv, "outer")
    hops = range(1, n_o // 2)
    sources = [lax.rem(node + n_o - 2 * hop, n_o) for hop in hops]
    parts = [lax.rem(group + n_g - turn, n_g) for turn in range(n_g)]
    where = [node * n_g, (node ^ 1) * n_g]
    for source in sources:
        where += [source * n_g, (source ^ 1) * n_g]
    shared_from = len(where)
    for source in sources:
        for part in parts:
            where += [source * n_g + part, (source ^ 1) * n_g + part]

    def cut(chunk):
        first_column, width = columns[chunk]
        if SHARED[chunk]:
            return lax.dynamic_slice(w_qkv, (group * depth, first_column), (depth, width))
        return w_qkv[:, first_column : first_column + width]

    def cross(array):
        return [shifted(array, "outer", 2 * hop) for hop in hops]

    def passed(chunk, arrived):
        turns = range(1, n_g if SHARED[chunk] else 1)
        return [[a] + [shifted(a, "groups", turn) for turn in turns] for a in arrived]

    def spread(chunk, arrived):
        pieces = [(w_qkv, 0), (beside, 1)]
        at = shared_from if SHARED[chunk] else 2
        for got in arrived:
            for array in got:
                pieces += [(array, at), (swapped(array, "outer"), at + 1)]
                at += 2
        return pieces

    def around(first, others):
        return [first] + [shifted(array, "inner", 1 + s) for s, array in enumerate(others)]

    normed = normalize(hidden, gain, n_o * n_g)

    counts = lax.dynamic_index_in_dim(loader_counts, node, 0, keepdims=False)
    inside = jnp.arange(rows, dtype=jnp.int32)
    spans = jnp.arange(n_i, dtype=jnp.int32)
    before = spans[:, None] < spans[None, :]
    mine_counts = lax.dynamic_index_in_dim(counts, me, 0, keepdims=False)
    sends = jnp.sum(jnp.where(before, mine_counts[:, None], 0), axis=0)
    takes = jnp.sum(jnp.where((spans < me)[:, None], counts, 0), axis=0)
    reached = (sends[None, :] + mine_counts[None, :]) <= inside[:, None]
    owner = jnp.sum(reached.astype(jnp.int32), axis=1)
    jump = jnp.sum(
        jnp.where(owner[:, None] == spans[None, :], (takes - sends + spans * rows)[None, :], 0), axis=1
    )
    packed = node * n_i * rows + inside + jump
    position = packed - doc_starts(boundaries, packed)
    half = HEAD_SIZE // 2
    frequency = ROPE_BASE ** (-(jnp.arange(half, dtype=jnp.float32) * 2.0 / HEAD_SIZE))
    angles = position.astype(jnp.float32)[:, None] * frequency[None, :]
    cosine, sine = jnp.cos(angles), jnp.sin(angles)
    turned = jnp.stack(
        [jnp.concatenate([cosine, cosine], axis=1), jnp.concatenate([-sine, sine], axis=1)]
    )
    table = jnp.stack([turned, jnp.stack([jnp.ones_like(turned[0]), jnp.zeros_like(turned[0])])])

    base = (node - 1) * n_i * rows
    starts = doc_starts(boundaries, (node * n_i + me) * rows + inside) - base
    ids = jnp.stack([node, me, starts[0]] + where).astype(jnp.int32)
    starts = starts[:, None]
    bias = bias[None]

    def projected(chunk, pieces, slots):
        first_column, width = columns[chunk]
        return project(
            ids, loader_counts, normed, table, bias, pieces, first_column, width, slots, n_i
        )

    arrived, normed, table, ids, starts, waiting = lax.optimization_barrier(
        (
            cross(cut(0)),
            normed,
            table,
            ids,
            starts,
            [cut(chunk) for chunk in range(1, len(columns))],
        )
    )
    crossing_value = cross(waiting[0])
    [key] = projected(0, spread(0, passed(0, arrived)), None)
    keys_held = around(key, [key] * (n_i - 1))

    crossing = cross(after(waiting[1], key))
    crossed, waiting, _ = lax.optimization_barrier((crossing_value, waiting, keys_held))
    [value] = projected(1, spread(1, passed(1, crossed)), None)
    values_held = around(value, [value] * (n_i - 1))
    stacked = jnp.stack(
        [jnp.concatenate(both, axis=1) for both in zip(keys_held, values_held)]
    )
    behind = from_behind(stacked, "outer")

    crossing, waiting, _ = lax.optimization_barrier((crossing, waiting, value))
    first, crossing = lax.optimization_barrier((passed(2, crossing), cross(waiting[2])))
    outs = projected(2, spread(2, after(first, stacked)), slot_rows)
    slots = [around(outs[0], outs[1:])]
    second = passed(3, crossing)
    keys, values = reorder(
        ids, loader_counts, after(stacked, outs[0], second), behind, slot_rows + 16
    )
    outs = projected(3, spread(3, after(second, slots[0][n_i // 2], keys)), slot_rows)
    slots.append(around(outs[0], outs[1:]))

    output = None
    at = 0
    for chunk, heads in enumerate(CHUNKS):
        output = attend(
            ids, loader_counts, starts, keys, values, slots[chunk], output, at, heads, TOGETHER[chunk]
        )
        at += heads
    return output


def solution(mesh):
    in_specs = (
        P(("groups", "outer", "inner"), None),
        P(),
        P("outer", None),
        P(),
        P("groups"),
        P("groups", None, None),
    )
    out_specs = P(("groups", "outer", "inner"), None)
    return jax.shard_map(
        on_device, mesh=mesh, in_specs=in_specs, out_specs=out_specs, check_vma=False
    )
```

```python
import functools
import math

import jax
import jax.numpy as jnp
from jax import lax
from jax.experimental import pallas as pl
from jax.experimental.pallas import tpu as pltpu
from jax.sharding import PartitionSpec as P

HEAD_SIZE = 128
HQ = 14
KEY_VALUE_HEADS = 2
QUERY_PER_KEY = 7
DOC_MOST = 1536
EPSILON = 1e-06
ROPE_BASE = 1000000.0
LEAST = -1e30
MASKED = -2e30
WIDTH_Q = HQ * HEAD_SIZE
WIDTH_K = KEY_VALUE_HEADS * HEAD_SIZE
TILE = 2 * HEAD_SIZE
CHUNKS = (8, 6)
TOGETHER = (4, 2)
SHARED = (False, False, True, True)
VMEM_LIMIT = 40 * 1024 * 1024


def shifted(array, axis, by):
    length = lax.axis_size(axis)
    return lax.ppermute(array, axis, [(i, (i + by) % length) for i in range(length)])


def swapped(array, axis):
    length = lax.axis_size(axis)
    return lax.ppermute(array, axis, [(i, i ^ 1) for i in range(length)])


def from_behind(array, axis):
    length = lax.axis_size(axis)
    return lax.ppermute(array, axis, [(i, i + 1) for i in range(length - 1)])


def after(value, *others):
    return lax.optimization_barrier((value, others))[0]


def doc_starts(boundaries, token_positions):
    doc_ends = boundaries[1:]
    lengths = doc_ends - boundaries[:-1]
    passed = doc_ends[None, :] <= token_positions[:, None]
    return jnp.sum(jnp.where(passed, lengths[None, :], 0), axis=1)


def smem():
    return pl.BlockSpec(memory_space=pltpu.SMEM)


def whole_block(shape):
    return pl.BlockSpec(shape, lambda *_: (0,) * len(shape))


def norm_kernel(x_ref, gain_ref, out_ref):
    x = x_ref[...].astype(jnp.float32)
    scale = lax.rsqrt(jnp.mean(x * x, axis=1, keepdims=True) + EPSILON)
    y = (x * scale * gain_ref[...]).astype(jnp.bfloat16)
    depth = out_ref.shape[2]
    for k in range(out_ref.shape[0]):
        out_ref[k] = y[:, k * depth : (k + 1) * depth]


def normalize(hidden, gain, pieces):
    rows, features = hidden.shape
    step = rows // 3
    return pl.pallas_call(
        norm_kernel,
        grid=(rows // step,),
        in_specs=[
            pl.BlockSpec((step, features), lambda r: (r, 0)),
            whole_block((1, features)),
        ],
        out_specs=pl.BlockSpec((pieces, step, features // pieces), lambda r: (0, r, 0)),
        out_shape=jax.ShapeDtypeStruct((pieces, rows, features // pieces), jnp.bfloat16),
        compiler_params=pltpu.CompilerParams(vmem_limit_bytes=VMEM_LIMIT),
        cost_estimate=pl.CostEstimate(
            flops=4 * rows * features, bytes_accessed=4 * rows * features, transcendentals=rows
        ),
    )(hidden, gain[None])


def rotate(tile, cosine, sine):
    parts = []
    for h in range(tile.shape[1] // HEAD_SIZE):
        x = tile[:, h * HEAD_SIZE : (h + 1) * HEAD_SIZE]
        parts.append(x * cosine + pltpu.roll(x, HEAD_SIZE // 2, 1) * sine)
    return jnp.concatenate(parts, axis=1)


def send_start(counts, node, loader, owner, length):
    total = jnp.int32(0)
    for d in range(length):
        total = total + jnp.where(d < owner, counts[node, loader, d], 0)
    return total


def take_start(counts, node, loader, owner, length):
    total = jnp.int32(0)
    for s in range(length):
        total = total + jnp.where(s < loader, counts[node, s, owner], 0)
    return total


def project_kernel(n_i, indices, splits, slots, ids, counts, normed, table, bias, *refs):
    weights, outs = refs[: len(indices)], refs[len(indices) :]
    total = None
    for (piece, weight, split) in zip(indices, weights, splits):
        depth = normed.shape[2]
        for part in range(split):
            at = ids[3 + piece] + part
            term = jnp.dot(
                normed[at],
                weight[part * depth : (part + 1) * depth, :],
                preferred_element_type=jnp.float32,
            )
            total = term if total is None else total + term
    tile = rotate(total + bias[...], table[0, 0], table[0, 1]).astype(jnp.bfloat16)
    if not slots:
        outs[0][...] = tile
        return
    node, me = ids[0], ids[1]
    slot_rows, rows = outs[0].shape[0], tile.shape[0]
    source = lax.broadcasted_iota(jnp.int32, (slot_rows, rows), 1) - lax.broadcasted_iota(
        jnp.int32, (slot_rows, rows), 0
    )
    for shift, out in enumerate(outs):
        owner = lax.rem(me + shift, n_i)
        start = send_start(counts, node, me, owner, n_i)
        pick = jnp.where(source == start, 1.0, 0.0).astype(jnp.bfloat16)
        out[...] = jnp.dot(pick, tile, preferred_element_type=jnp.float32).astype(jnp.bfloat16)


def project(ids, counts, normed, table, bias, pieces, first_column, width, slot_rows, n_i):
    rows = normed.shape[1]
    depth = normed.shape[2]
    base = first_column // TILE
    weights = [p[0] for p in pieces]
    splits = tuple(w.shape[0] // depth for w in weights)
    offsets = [base if p[1] < 2 else 0 for p in pieces]
    slots = slot_rows is not None
    if slots:
        out_shape = [jax.ShapeDtypeStruct((slot_rows, width), jnp.bfloat16)] * n_i
        out_specs = [pl.BlockSpec((slot_rows, TILE), lambda c: (0, c))] * n_i
        table_spec = pl.BlockSpec((1, 2, rows, HEAD_SIZE), lambda c: (0, 0, 0, 0))
    else:
        out_shape = [jax.ShapeDtypeStruct((rows, width), jnp.bfloat16)]
        out_specs = [pl.BlockSpec((rows, TILE), lambda c: (0, c))]
        still = first_column // (WIDTH_Q + WIDTH_K)
        table_spec = pl.BlockSpec((1, 2, rows, HEAD_SIZE), lambda c: (still, 0, 0, 0))
    features = normed.shape[0] * depth
    return pl.pallas_call(
        functools.partial(project_kernel, n_i, tuple(p[1] for p in pieces), splits, slots),
        grid=(width // TILE,),
        in_specs=[
            smem(),
            smem(),
            whole_block(normed.shape),
            table_spec,
            pl.BlockSpec((1, TILE), lambda c: (0, base + c)),
        ]
        + [
            pl.BlockSpec((w.shape[0], TILE), functools.partial(lambda off, c: (0, off + c), off))
            for w, off in zip(weights, offsets)
        ],
        out_specs=out_specs,
        out_shape=out_shape,
        compiler_params=pltpu.CompilerParams(vmem_limit_bytes=VMEM_LIMIT),
        cost_estimate=pl.CostEstimate(
            flops=2 * rows * features * width,
            bytes_accessed=2 * features * (rows + width),
            transcendentals=0,
        ),
    )(ids, counts, normed, table, bias, *weights)


def reorder_kernel(n_i, reach, ids, counts, held, behind, keys_out, values_out):
    block = pl.program_id(0)
    node, me, first = ids[0], ids[1], ids[2]
    rows = held.shape[1]

    @pl.when((block >= first // rows) & (block <= n_i + me))
    def _():
        place = lax.broadcasted_iota(jnp.int32, (rows, reach), 0)
        gap = lax.broadcasted_iota(jnp.int32, (rows, reach), 1) - place

        def gather(arrived, which, owner):
            total = None
            for shift in range(n_i):
                loader = lax.rem(me + n_i - shift, n_i)
                start = take_start(counts, which, loader, owner, n_i)
                end = start + counts[which, loader, owner]
                source = send_start(counts, which, loader, owner, n_i)
                at = pl.multiple_of(jnp.minimum(source // 16 * 16, rows - reach), 16)
                hit = (gap == source - start - at) & (place >= start) & (place < end)
                pick = jnp.where(hit, 1.0, 0.0).astype(jnp.bfloat16)
                term = jnp.dot(
                    pick, arrived[shift, pl.ds(at, reach), :], preferred_element_type=jnp.float32
                )
                total = term if total is None else total + term
            keys_out[0] = total[:, :WIDTH_K].T.astype(jnp.bfloat16)
            values_out[0] = total[:, WIDTH_K:].astype(jnp.bfloat16)

        @pl.when(block < n_i)
        def _():
            gather(behind, jnp.maximum(node - 1, 0), block)

        @pl.when(block >= n_i)
        def _():
            gather(held, node, block - n_i)


def reorder(ids, counts, held, behind, reach):
    n_i, rows, width = held.shape
    return pl.pallas_call(
        functools.partial(reorder_kernel, n_i, reach),
        grid=(2 * n_i,),
        in_specs=[smem(), smem(), whole_block(held.shape), whole_block(held.shape)],
        out_specs=[
            pl.BlockSpec((1, WIDTH_K, rows), lambda b: (b, 0, 0)),
            pl.BlockSpec((1, rows, WIDTH_K), lambda b: (b, 0, 0)),
        ],
        out_shape=[
            jax.ShapeDtypeStruct((2 * n_i, WIDTH_K, rows), jnp.bfloat16),
            jax.ShapeDtypeStruct((2 * n_i, rows, WIDTH_K), jnp.bfloat16),
        ],
        compiler_params=pltpu.CompilerParams(vmem_limit_bytes=VMEM_LIMIT),
        cost_estimate=pl.CostEstimate(
            flops=2 * (n_i + 1) * n_i * rows * rows * width,
            bytes_accessed=8 * n_i * rows * width,
            transcendentals=0,
        ),
    )(ids, counts, held, behind)


def attend_kernel(n_i, first_head, heads, pair, ids, counts, starts, keys, values, *refs):
    slots, refs = refs[:n_i], refs[-8:]
    out, queries, bias, scores, peak, highest, total, summed = refs
    node, me, first = ids[0], ids[1], ids[2]
    rows = out.shape[0]
    slot_rows = slots[0].shape[0]
    at = pl.program_id(0)
    low, high = first // rows, n_i + me + 1
    factor = math.log2(math.e) / math.sqrt(HEAD_SIZE)

    @pl.when(at == 0)
    def _():
        place = lax.broadcasted_iota(jnp.int32, (rows, slot_rows), 0)
        inside = lax.broadcasted_iota(jnp.int32, (rows, slot_rows), 1)
        gathered = None
        for shift in range(n_i):
            loader = lax.rem(me + n_i - shift, n_i)
            start = take_start(counts, node, loader, me, n_i)
            hit = (place - inside == start) & (inside < counts[node, loader, me])
            pick = jnp.where(hit, 1.0, 0.0).astype(jnp.bfloat16)
            term = jnp.dot(pick, slots[shift][...], preferred_element_type=jnp.float32)
            gathered = term if gathered is None else gathered + term
        gathered = gathered.astype(jnp.bfloat16)
        for head in range(heads):
            queries[head] = gathered[:, head * HEAD_SIZE : (head + 1) * HEAD_SIZE]
        ahead = lax.broadcasted_iota(jnp.int32, (rows, rows), 1)
        row = lax.broadcasted_iota(jnp.int32, (rows, rows), 0)

        def shade(block, carry):
            seen = (ahead >= starts[...] - block * rows) & (
                ahead - row <= (n_i + me - block) * rows
            )
            bias[block - low] = jnp.where(seen, 0.0, MASKED)
            return carry

        lax.fori_loop(low, high, shade, 0)

    def runs(step):
        found = []
        for j in range(pair):
            group = (first_head + step * pair + j) // QUERY_PER_KEY
            if found and found[-1][2] == group:
                found[-1][1] += 1
            else:
                found.append([j, 1, group])
        return found

    def run(index):
        form, weigh = index < heads // pair, index > 0
        now, then = index % 2, (index + 1) % 2
        if form:
            peak[now] = jnp.full(peak.shape[1:], LEAST, jnp.float32)
        if weigh:
            top = jnp.max(peak[then], axis=2, keepdims=True) * factor
            highest[...] = jnp.broadcast_to(top, highest.shape)
            total[...] = jnp.zeros(total.shape, jnp.float32)
            summed[...] = jnp.zeros(summed.shape, jnp.float32)

        def step(block, carry):
            for j, many, group in runs(index) if form else ():
                at = slice(j, j + many)
                key = keys[block, group * HEAD_SIZE : (group + 1) * HEAD_SIZE, :]
                query = queries[index * pair + j : index * pair + j + many]
                score = jnp.dot(
                    query.reshape(many * rows, HEAD_SIZE), key, preferred_element_type=jnp.float32
                ).reshape(many, rows, rows)
                score = score + bias[block - low][None]
                scores[now, at, block - low] = score
                best = peak[now, at]
                for k in range(rows // HEAD_SIZE):
                    best = jnp.maximum(best, score[:, :, k * HEAD_SIZE : (k + 1) * HEAD_SIZE])
                peak[now, at] = best
            for j, many, group in runs(index - 1) if weigh else ():
                at = slice(j, j + many)
                value = values[block, :, group * HEAD_SIZE : (group + 1) * HEAD_SIZE]
                weights = []
                add = total[at]
                for k in range(rows // HEAD_SIZE):
                    lane = slice(k * HEAD_SIZE, (k + 1) * HEAD_SIZE)
                    weight = jnp.exp2(scores[then, at, block - low, :, lane] * factor - highest[at])
                    add = add + weight
                    weights.append(weight.astype(jnp.bfloat16))
                total[at] = add
                weights = jnp.concatenate(weights, axis=2).reshape(many * rows, rows)
                summed[at] += jnp.dot(
                    weights, value, preferred_element_type=jnp.float32
                ).reshape(many, rows, HEAD_SIZE)
            return carry

        lax.fori_loop(low, high, step, 0)
        if weigh:
            for j in range(pair):
                whole = jnp.sum(total[j], axis=1, keepdims=True)
                out[:, j * HEAD_SIZE : (j + 1) * HEAD_SIZE] = (summed[j] / whole).astype(
                    jnp.bfloat16
                )

    for index in range(heads // pair + 1):
        pl.when(at == index)(functools.partial(run, index))


def attend(ids, counts, starts, keys, values, slots, before, first_head, heads, pair):
    rows = starts.shape[0]
    n_i = len(slots)
    slot_rows, width = slots[0].shape
    aliased = before is not None
    wide = (rows, HEAD_SIZE)
    blocks = (DOC_MOST + rows - 2) // rows + 1
    return pl.pallas_call(
        functools.partial(attend_kernel, n_i, first_head, heads, pair),
        grid=(heads // pair + 1,),
        in_specs=[
            smem(),
            smem(),
            whole_block(starts.shape),
            whole_block(keys.shape),
            whole_block(values.shape),
        ]
        + [whole_block((slot_rows, width))] * n_i
        + ([pl.BlockSpec(memory_space=pl.ANY)] if aliased else []),
        out_specs=pl.BlockSpec(
            (rows, pair * HEAD_SIZE), lambda h: (0, first_head // pair + jnp.maximum(h - 1, 0))
        ),
        out_shape=jax.ShapeDtypeStruct((rows, WIDTH_Q), jnp.bfloat16),
        scratch_shapes=[
            pltpu.VMEM((heads, *wide), jnp.bfloat16),
            pltpu.VMEM((blocks, rows, rows), jnp.float32),
            pltpu.VMEM((2, pair, blocks, rows, rows), jnp.float32),
            pltpu.VMEM((2, pair, *wide), jnp.float32),
            pltpu.VMEM((pair, *wide), jnp.float32),
            pltpu.VMEM((pair, *wide), jnp.float32),
            pltpu.VMEM((pair, *wide), jnp.float32),
        ],
        input_output_aliases={5 + n_i: 0} if aliased else {},
        compiler_params=pltpu.CompilerParams(vmem_limit_bytes=VMEM_LIMIT),
        cost_estimate=pl.CostEstimate(
            flops=16 * heads * rows * rows * HEAD_SIZE,
            bytes_accessed=keys.size * 4,
            transcendentals=4 * heads * rows * rows,
        ),
    )(ids, counts, starts, keys, values, *slots, *([before] if aliased else []))


def on_device(hidden, gain, w_qkv, bias, boundaries, loader_counts):
    rows = hidden.shape[0]
    n_g, n_o, n_i = (lax.axis_size(a) for a in ("groups", "outer", "inner"))
    group, node, me = (lax.axis_index(a) for a in ("groups", "outer", "inner"))
    depth = w_qkv.shape[0] // n_g
    slot_rows = rows // n_i + rows // n_i // 2
    slot_rows = (slot_rows + 15) // 16 * 16

    columns = [(WIDTH_Q, WIDTH_K), (WIDTH_Q + WIDTH_K, WIDTH_K)]
    at = 0
    for heads in CHUNKS:
        columns.append((at * HEAD_SIZE, heads * HEAD_SIZE))
        at += heads
    beside = swapped(w_qkv, "outer")
    hops = range(1, n_o // 2)
    sources = [lax.rem(node + n_o - 2 * hop, n_o) for hop in hops]
    parts = [lax.rem(group + n_g - turn, n_g) for turn in range(n_g)]
    where = [node * n_g, (node ^ 1) * n_g]
    for source in sources:
        where += [source * n_g, (source ^ 1) * n_g]
    shared_from = len(where)
    for source in sources:
        for part in parts:
            where += [source * n_g + part, (source ^ 1) * n_g + part]

    def cut(chunk):
        first_column, width = columns[chunk]
        if SHARED[chunk]:
            return lax.dynamic_slice(w_qkv, (group * depth, first_column), (depth, width))
        return w_qkv[:, first_column : first_column + width]

    def cross(array):
        return [shifted(array, "outer", 2 * hop) for hop in hops]

    def passed(chunk, arrived):
        turns = range(1, n_g if SHARED[chunk] else 1)
        return [[a] + [shifted(a, "groups", turn) for turn in turns] for a in arrived]

    def spread(chunk, arrived):
        pieces = [(w_qkv, 0), (beside, 1)]
        at = shared_from if SHARED[chunk] else 2
        for got in arrived:
            for array in got:
                pieces += [(array, at), (swapped(array, "outer"), at + 1)]
                at += 2
        return pieces

    def around(first, others):
        return [first] + [shifted(array, "inner", 1 + s) for s, array in enumerate(others)]

    normed = normalize(hidden, gain, n_o * n_g)

    counts = lax.dynamic_index_in_dim(loader_counts, node, 0, keepdims=False)
    inside = jnp.arange(rows, dtype=jnp.int32)
    spans = jnp.arange(n_i, dtype=jnp.int32)
    before = spans[:, None] < spans[None, :]
    mine_counts = lax.dynamic_index_in_dim(counts, me, 0, keepdims=False)
    sends = jnp.sum(jnp.where(before, mine_counts[:, None], 0), axis=0)
    takes = jnp.sum(jnp.where((spans < me)[:, None], counts, 0), axis=0)
    reached = (sends[None, :] + mine_counts[None, :]) <= inside[:, None]
    owner = jnp.sum(reached.astype(jnp.int32), axis=1)
    jump = jnp.sum(
        jnp.where(owner[:, None] == spans[None, :], (takes - sends + spans * rows)[None, :], 0), axis=1
    )
    packed = node * n_i * rows + inside + jump
    position = packed - doc_starts(boundaries, packed)
    half = HEAD_SIZE // 2
    frequency = ROPE_BASE ** (-(jnp.arange(half, dtype=jnp.float32) * 2.0 / HEAD_SIZE))
    angles = position.astype(jnp.float32)[:, None] * frequency[None, :]
    cosine, sine = jnp.cos(angles), jnp.sin(angles)
    turned = jnp.stack(
        [jnp.concatenate([cosine, cosine], axis=1), jnp.concatenate([-sine, sine], axis=1)]
    )
    table = jnp.stack([turned, jnp.stack([jnp.ones_like(turned[0]), jnp.zeros_like(turned[0])])])

    base = (node - 1) * n_i * rows
    starts = doc_starts(boundaries, (node * n_i + me) * rows + inside) - base
    ids = jnp.stack([node, me, starts[0]] + where).astype(jnp.int32)
    starts = starts[:, None]
    bias = bias[None]

    def projected(chunk, pieces, slots):
        first_column, width = columns[chunk]
        return project(
            ids, loader_counts, normed, table, bias, pieces, first_column, width, slots, n_i
        )

    arrived, normed, table, ids, starts, waiting = lax.optimization_barrier(
        (
            cross(cut(0)),
            normed,
            table,
            ids,
            starts,
            [cut(chunk) for chunk in range(1, len(columns))],
        )
    )
    crossing_value = cross(waiting[0])
    [key] = projected(0, spread(0, passed(0, arrived)), None)
    keys_held = around(key, [key] * (n_i - 1))

    crossing = cross(after(waiting[1], key))
    crossed, waiting, _ = lax.optimization_barrier((crossing_value, waiting, keys_held))
    [value] = projected(1, spread(1, passed(1, crossed)), None)
    values_held = around(value, [value] * (n_i - 1))
    stacked = jnp.stack(
        [jnp.concatenate(both, axis=1) for both in zip(keys_held, values_held)]
    )
    behind = from_behind(stacked, "outer")

    crossing, waiting, _ = lax.optimization_barrier((crossing, waiting, value))
    first, crossing = lax.optimization_barrier((passed(2, crossing), cross(waiting[2])))
    outs = projected(2, spread(2, after(first, stacked)), slot_rows)
    slots = [around(outs[0], outs[1:])]
    second = passed(3, crossing)
    keys, values = reorder(
        ids, loader_counts, after(stacked, outs[0], second), behind, slot_rows + 16
    )
    outs = projected(3, spread(3, after(second, slots[0][n_i // 2], keys)), slot_rows)
    slots.append(around(outs[0], outs[1:]))

    output = None
    at = 0
    for chunk, heads in enumerate(CHUNKS):
        output = attend(
            ids, loader_counts, starts, keys, values, slots[chunk], output, at, heads, TOGETHER[chunk]
        )
        at += heads
    return output


def solution(mesh):
    in_specs = (
        P(("groups", "outer", "inner"), None),
        P(),
        P("outer", None),
        P(),
        P("groups"),
        P("groups", None, None),
    )
    out_specs = P(("groups", "outer", "inner"), None)
    return jax.shard_map(
        on_device, mesh=mesh, in_specs=in_specs, out_specs=out_specs, check_vma=False
    )
```

```python
import functools
import math

import jax
import jax.numpy as jnp
from jax import lax
from jax.experimental import pallas as pl
from jax.experimental.pallas import tpu as pltpu
from jax.sharding import PartitionSpec as P

HEAD_SIZE = 128
HQ = 14
KEY_VALUE_HEADS = 2
QUERY_PER_KEY = 7
DOC_MOST = 1536
EPSILON = 1e-06
ROPE_BASE = 1000000.0
LEAST = -1e30
MASKED = -2e30
WIDTH_Q = HQ * HEAD_SIZE
WIDTH_K = KEY_VALUE_HEADS * HEAD_SIZE
TILE = 2 * HEAD_SIZE
CHUNKS = (8, 6)
TOGETHER = (4, 2)
SHARED = (False, False, True, True)
VMEM_LIMIT = 40 * 1024 * 1024


def shifted(array, axis, by):
    length = lax.axis_size(axis)
    return lax.ppermute(array, axis, [(i, (i + by) % length) for i in range(length)])


def swapped(array, axis):
    length = lax.axis_size(axis)
    return lax.ppermute(array, axis, [(i, i ^ 1) for i in range(length)])


def from_behind(array, axis):
    length = lax.axis_size(axis)
    return lax.ppermute(array, axis, [(i, i + 1) for i in range(length - 1)])


def after(value, *others):
    return lax.optimization_barrier((value, others))[0]


def doc_starts(boundaries, token_positions):
    doc_ends = boundaries[1:]
    lengths = doc_ends - boundaries[:-1]
    passed = doc_ends[None, :] <= token_positions[:, None]
    return jnp.sum(jnp.where(passed, lengths[None, :], 0), axis=1)


def smem():
    return pl.BlockSpec(memory_space=pltpu.SMEM)


def whole_block(shape):
    return pl.BlockSpec(shape, lambda *_: (0,) * len(shape))


def norm_kernel(x_ref, gain_ref, out_ref):
    x = x_ref[...].astype(jnp.float32)
    scale = lax.rsqrt(jnp.mean(x * x, axis=1, keepdims=True) + EPSILON)
    y = (x * scale * gain_ref[...]).astype(jnp.bfloat16)
    depth = out_ref.shape[2]
    for k in range(out_ref.shape[0]):
        out_ref[k] = y[:, k * depth : (k + 1) * depth]


def normalize(hidden, gain, pieces):
    rows, features = hidden.shape
    step = rows // 3
    return pl.pallas_call(
        norm_kernel,
        grid=(rows // step,),
        in_specs=[
            pl.BlockSpec((step, features), lambda r: (r, 0)),
            whole_block((1, features)),
        ],
        out_specs=pl.BlockSpec((pieces, step, features // pieces), lambda r: (0, r, 0)),
        out_shape=jax.ShapeDtypeStruct((pieces, rows, features // pieces), jnp.bfloat16),
        compiler_params=pltpu.CompilerParams(vmem_limit_bytes=VMEM_LIMIT),
        cost_estimate=pl.CostEstimate(
            flops=4 * rows * features, bytes_accessed=4 * rows * features, transcendentals=rows
        ),
    )(hidden, gain[None])


def rotate(tile, cosine, sine):
    parts = []
    for h in range(tile.shape[1] // HEAD_SIZE):
        x = tile[:, h * HEAD_SIZE : (h + 1) * HEAD_SIZE]
        parts.append(x * cosine + pltpu.roll(x, HEAD_SIZE // 2, 1) * sine)
    return jnp.concatenate(parts, axis=1)


def send_start(counts, node, loader, owner, length):
    total = jnp.int32(0)
    for d in range(length):
        total = total + jnp.where(d < owner, counts[node, loader, d], 0)
    return total


def take_start(counts, node, loader, owner, length):
    total = jnp.int32(0)
    for s in range(length):
        total = total + jnp.where(s < loader, counts[node, s, owner], 0)
    return total


def project_kernel(n_i, indices, splits, slots, ids, counts, normed, table, bias, *refs):
    weights, outs = refs[: len(indices)], refs[len(indices) :]
    total = None
    for (piece, weight, split) in zip(indices, weights, splits):
        depth = normed.shape[2]
        for part in range(split):
            at = ids[3 + piece] + part
            term = jnp.dot(
                normed[at],
                weight[part * depth : (part + 1) * depth, :],
                preferred_element_type=jnp.float32,
            )
            total = term if total is None else total + term
    tile = rotate(total + bias[...], table[0, 0], table[0, 1]).astype(jnp.bfloat16)
    if not slots:
        outs[0][...] = tile
        return
    node, me = ids[0], ids[1]
    slot_rows, rows = outs[0].shape[0], tile.shape[0]
    source = lax.broadcasted_iota(jnp.int32, (slot_rows, rows), 1) - lax.broadcasted_iota(
        jnp.int32, (slot_rows, rows), 0
    )
    for shift, out in enumerate(outs):
        owner = lax.rem(me + shift, n_i)
        start = send_start(counts, node, me, owner, n_i)
        pick = jnp.where(source == start, 1.0, 0.0).astype(jnp.bfloat16)
        out[...] = jnp.dot(pick, tile, preferred_element_type=jnp.float32).astype(jnp.bfloat16)


def project(ids, counts, normed, table, bias, pieces, first_column, width, slot_rows, n_i):
    rows = normed.shape[1]
    depth = normed.shape[2]
    base = first_column // TILE
    weights = [p[0] for p in pieces]
    splits = tuple(w.shape[0] // depth for w in weights)
    offsets = [base if p[1] < 2 else 0 for p in pieces]
    slots = slot_rows is not None
    if slots:
        out_shape = [jax.ShapeDtypeStruct((slot_rows, width), jnp.bfloat16)] * n_i
        out_specs = [pl.BlockSpec((slot_rows, TILE), lambda c: (0, c))] * n_i
        table_spec = pl.BlockSpec((1, 2, rows, HEAD_SIZE), lambda c: (0, 0, 0, 0))
    else:
        out_shape = [jax.ShapeDtypeStruct((rows, width), jnp.bfloat16)]
        out_specs = [pl.BlockSpec((rows, TILE), lambda c: (0, c))]
        still = first_column // (WIDTH_Q + WIDTH_K)
        table_spec = pl.BlockSpec((1, 2, rows, HEAD_SIZE), lambda c: (still, 0, 0, 0))
    features = normed.shape[0] * depth
    return pl.pallas_call(
        functools.partial(project_kernel, n_i, tuple(p[1] for p in pieces), splits, slots),
        grid=(width // TILE,),
        in_specs=[
            smem(),
            smem(),
            whole_block(normed.shape),
            table_spec,
            pl.BlockSpec((1, TILE), lambda c: (0, base + c)),
        ]
        + [
            pl.BlockSpec((w.shape[0], TILE), functools.partial(lambda off, c: (0, off + c), off))
            for w, off in zip(weights, offsets)
        ],
        out_specs=out_specs,
        out_shape=out_shape,
        compiler_params=pltpu.CompilerParams(vmem_limit_bytes=VMEM_LIMIT),
        cost_estimate=pl.CostEstimate(
            flops=2 * rows * features * width,
            bytes_accessed=2 * features * (rows + width),
            transcendentals=0,
        ),
    )(ids, counts, normed, table, bias, *weights)


def reorder_kernel(n_i, reach, ids, counts, held, behind, keys_out, values_out):
    block = pl.program_id(0)
    node, me, first = ids[0], ids[1], ids[2]
    rows = held.shape[1]

    @pl.when((block >= first // rows) & (block <= n_i + me))
    def _():
        place = lax.broadcasted_iota(jnp.int32, (rows, reach), 0)
        gap = lax.broadcasted_iota(jnp.int32, (rows, reach), 1) - place

        def gather(arrived, which, owner):
            total = None
            for shift in range(n_i):
                loader = lax.rem(me + n_i - shift, n_i)
                start = take_start(counts, which, loader, owner, n_i)
                end = start + counts[which, loader, owner]
                source = send_start(counts, which, loader, owner, n_i)
                at = pl.multiple_of(jnp.minimum(source // 16 * 16, rows - reach), 16)
                hit = (gap == source - start - at) & (place >= start) & (place < end)
                pick = jnp.where(hit, 1.0, 0.0).astype(jnp.bfloat16)
                term = jnp.dot(
                    pick, arrived[shift, pl.ds(at, reach), :], preferred_element_type=jnp.float32
                )
                total = term if total is None else total + term
            keys_out[0] = total[:, :WIDTH_K].T.astype(jnp.bfloat16)
            values_out[0] = total[:, WIDTH_K:].astype(jnp.bfloat16)

        @pl.when(block < n_i)
        def _():
            gather(behind, jnp.maximum(node - 1, 0), block)

        @pl.when(block >= n_i)
        def _():
            gather(held, node, block - n_i)


def reorder(ids, counts, held, behind, reach):
    n_i, rows, width = held.shape
    return pl.pallas_call(
        functools.partial(reorder_kernel, n_i, reach),
        grid=(2 * n_i,),
        in_specs=[smem(), smem(), whole_block(held.shape), whole_block(held.shape)],
        out_specs=[
            pl.BlockSpec((1, WIDTH_K, rows), lambda b: (b, 0, 0)),
            pl.BlockSpec((1, rows, WIDTH_K), lambda b: (b, 0, 0)),
        ],
        out_shape=[
            jax.ShapeDtypeStruct((2 * n_i, WIDTH_K, rows), jnp.bfloat16),
            jax.ShapeDtypeStruct((2 * n_i, rows, WIDTH_K), jnp.bfloat16),
        ],
        compiler_params=pltpu.CompilerParams(vmem_limit_bytes=VMEM_LIMIT),
        cost_estimate=pl.CostEstimate(
            flops=2 * (n_i + 1) * n_i * rows * rows * width,
            bytes_accessed=8 * n_i * rows * width,
            transcendentals=0,
        ),
    )(ids, counts, held, behind)


def attend_kernel(n_i, first_head, heads, pair, ids, counts, starts, keys, values, *refs):
    slots, refs = refs[:n_i], refs[-8:]
    out, queries, bias, scores, peak, highest, total, summed = refs
    node, me, first = ids[0], ids[1], ids[2]
    rows = out.shape[0]
    slot_rows = slots[0].shape[0]
    at = pl.program_id(0)
    low, high = first // rows, n_i + me + 1
    factor = math.log2(math.e) / math.sqrt(HEAD_SIZE)

    @pl.when(at == 0)
    def _():
        place = lax.broadcasted_iota(jnp.int32, (rows, slot_rows), 0)
        inside = lax.broadcasted_iota(jnp.int32, (rows, slot_rows), 1)
        gathered = None
        for shift in range(n_i):
            loader = lax.rem(me + n_i - shift, n_i)
            start = take_start(counts, node, loader, me, n_i)
            hit = (place - inside == start) & (inside < counts[node, loader, me])
            pick = jnp.where(hit, 1.0, 0.0).astype(jnp.bfloat16)
            term = jnp.dot(pick, slots[shift][...], preferred_element_type=jnp.float32)
            gathered = term if gathered is None else gathered + term
        gathered = gathered.astype(jnp.bfloat16)
        for head in range(heads):
            queries[head] = gathered[:, head * HEAD_SIZE : (head + 1) * HEAD_SIZE]
        ahead = lax.broadcasted_iota(jnp.int32, (rows, rows), 1)
        row = lax.broadcasted_iota(jnp.int32, (rows, rows), 0)

        def shade(block, carry):
            seen = (ahead >= starts[...] - block * rows) & (
                ahead - row <= (n_i + me - block) * rows
            )
            bias[block - low] = jnp.where(seen, 0.0, MASKED)
            return carry

        lax.fori_loop(low, high, shade, 0)

    def runs(step):
        found = []
        for j in range(pair):
            group = (first_head + step * pair + j) // QUERY_PER_KEY
            if found and found[-1][2] == group:
                found[-1][1] += 1
            else:
                found.append([j, 1, group])
        return found

    def run(index):
        form, weigh = index < heads // pair, index > 0
        now, then = index % 2, (index + 1) % 2
        if form:
            peak[now] = jnp.full(peak.shape[1:], LEAST, jnp.float32)
        if weigh:
            top = jnp.max(peak[then], axis=2, keepdims=True) * factor
            highest[...] = jnp.broadcast_to(top, highest.shape)
            total[...] = jnp.zeros(total.shape, jnp.float32)
            summed[...] = jnp.zeros(summed.shape, jnp.float32)

        def step(block, carry):
            for j, many, group in runs(index) if form else ():
                at = slice(j, j + many)
                key = keys[block, group * HEAD_SIZE : (group + 1) * HEAD_SIZE, :]
                query = queries[index * pair + j : index * pair + j + many]
                score = jnp.dot(
                    query.reshape(many * rows, HEAD_SIZE), key, preferred_element_type=jnp.float32
                ).reshape(many, rows, rows)
                score = score + bias[block - low][None]
                scores[now, at, block - low] = score
                best = peak[now, at]
                for k in range(rows // HEAD_SIZE):
                    best = jnp.maximum(best, score[:, :, k * HEAD_SIZE : (k + 1) * HEAD_SIZE])
                peak[now, at] = best
            for j, many, group in runs(index - 1) if weigh else ():
                at = slice(j, j + many)
                value = values[block, :, group * HEAD_SIZE : (group + 1) * HEAD_SIZE]
                weights = []
                add = total[at]
                for k in range(rows // HEAD_SIZE):
                    lane = slice(k * HEAD_SIZE, (k + 1) * HEAD_SIZE)
                    weight = jnp.exp2(scores[then, at, block - low, :, lane] * factor - highest[at])
                    add = add + weight
                    weights.append(weight.astype(jnp.bfloat16))
                total[at] = add
                weights = jnp.concatenate(weights, axis=2).reshape(many * rows, rows)
                summed[at] += jnp.dot(
                    weights, value, preferred_element_type=jnp.float32
                ).reshape(many, rows, HEAD_SIZE)
            return carry

        lax.fori_loop(low, high, step, 0)
        if weigh:
            for j in range(pair):
                whole = jnp.sum(total[j], axis=1, keepdims=True)
                out[:, j * HEAD_SIZE : (j + 1) * HEAD_SIZE] = (summed[j] / whole).astype(
                    jnp.bfloat16
                )

    for index in range(heads // pair + 1):
        pl.when(at == index)(functools.partial(run, index))


def attend(ids, counts, starts, keys, values, slots, before, first_head, heads, pair):
    rows = starts.shape[0]
    n_i = len(slots)
    slot_rows, width = slots[0].shape
    aliased = before is not None
    wide = (rows, HEAD_SIZE)
    blocks = (DOC_MOST + rows - 2) // rows + 1
    return pl.pallas_call(
        functools.partial(attend_kernel, n_i, first_head, heads, pair),
        grid=(heads // pair + 1,),
        in_specs=[
            smem(),
            smem(),
            whole_block(starts.shape),
            whole_block(keys.shape),
            whole_block(values.shape),
        ]
        + [whole_block((slot_rows, width))] * n_i
        + ([pl.BlockSpec(memory_space=pl.ANY)] if aliased else []),
        out_specs=pl.BlockSpec(
            (rows, pair * HEAD_SIZE), lambda h: (0, first_head // pair + jnp.maximum(h - 1, 0))
        ),
        out_shape=jax.ShapeDtypeStruct((rows, WIDTH_Q), jnp.bfloat16),
        scratch_shapes=[
            pltpu.VMEM((heads, *wide), jnp.bfloat16),
            pltpu.VMEM((blocks, rows, rows), jnp.float32),
            pltpu.VMEM((2, pair, blocks, rows, rows), jnp.float32),
            pltpu.VMEM((2, pair, *wide), jnp.float32),
            pltpu.VMEM((pair, *wide), jnp.float32),
            pltpu.VMEM((pair, *wide), jnp.float32),
            pltpu.VMEM((pair, *wide), jnp.float32),
        ],
        input_output_aliases={5 + n_i: 0} if aliased else {},
        compiler_params=pltpu.CompilerParams(vmem_limit_bytes=VMEM_LIMIT),
        cost_estimate=pl.CostEstimate(
            flops=16 * heads * rows * rows * HEAD_SIZE,
            bytes_accessed=keys.size * 4,
            transcendentals=4 * heads * rows * rows,
        ),
    )(ids, counts, starts, keys, values, *slots, *([before] if aliased else []))


def on_device(hidden, gain, w_qkv, bias, boundaries, loader_counts):
    rows = hidden.shape[0]
    n_g, n_o, n_i = (lax.axis_size(a) for a in ("groups", "outer", "inner"))
    group, node, me = (lax.axis_index(a) for a in ("groups", "outer", "inner"))
    depth = w_qkv.shape[0] // n_g
    slot_rows = rows // n_i + rows // n_i // 2
    slot_rows = (slot_rows + 15) // 16 * 16

    columns = [(WIDTH_Q, WIDTH_K), (WIDTH_Q + WIDTH_K, WIDTH_K)]
    at = 0
    for heads in CHUNKS:
        columns.append((at * HEAD_SIZE, heads * HEAD_SIZE))
        at += heads
    beside = swapped(w_qkv, "outer")
    hops = range(1, n_o // 2)
    sources = [lax.rem(node + n_o - 2 * hop, n_o) for hop in hops]
    parts = [lax.rem(group + n_g - turn, n_g) for turn in range(n_g)]
    where = [node * n_g, (node ^ 1) * n_g]
    for source in sources:
        where += [source * n_g, (source ^ 1) * n_g]
    shared_from = len(where)
    for source in sources:
        for part in parts:
            where += [source * n_g + part, (source ^ 1) * n_g + part]

    def cut(chunk, array=w_qkv):
        first_column, width = columns[chunk]
        if SHARED[chunk]:
            return lax.dynamic_slice(array, (group * depth, first_column), (depth, width))
        return array[:, first_column : first_column + width]

    def cross(array):
        return [shifted(array, "outer", 2 * hop) for hop in hops]

    def passed(chunk, arrived):
        turns = range(1, n_g if SHARED[chunk] else 1)
        return [[a] + [shifted(a, "groups", turn) for turn in turns] for a in arrived]

    def spread(chunk, arrived, sent=None):
        pieces = [(w_qkv, 0), (beside, 1)]
        at = shared_from if SHARED[chunk] else 2
        for hop, got in enumerate(arrived):
            for turn, array in enumerate(got):
                other = sent[hop] if sent and turn == 0 else swapped(array, "outer")
                pieces += [(array, at), (other, at + 1)]
                at += 2
        return pieces

    def around(first, others):
        return [first] + [shifted(array, "inner", 1 + s) for s, array in enumerate(others)]

    normed = normalize(hidden, gain, n_o * n_g)

    counts = lax.dynamic_index_in_dim(loader_counts, node, 0, keepdims=False)
    inside = jnp.arange(rows, dtype=jnp.int32)
    spans = jnp.arange(n_i, dtype=jnp.int32)
    before = spans[:, None] < spans[None, :]
    mine_counts = lax.dynamic_index_in_dim(counts, me, 0, keepdims=False)
    sends = jnp.sum(jnp.where(before, mine_counts[:, None], 0), axis=0)
    takes = jnp.sum(jnp.where((spans < me)[:, None], counts, 0), axis=0)
    reached = (sends[None, :] + mine_counts[None, :]) <= inside[:, None]
    owner = jnp.sum(reached.astype(jnp.int32), axis=1)
    jump = jnp.sum(
        jnp.where(owner[:, None] == spans[None, :], (takes - sends + spans * rows)[None, :], 0), axis=1
    )
    packed = node * n_i * rows + inside + jump
    position = packed - doc_starts(boundaries, packed)
    half = HEAD_SIZE // 2
    frequency = ROPE_BASE ** (-(jnp.arange(half, dtype=jnp.float32) * 2.0 / HEAD_SIZE))
    angles = position.astype(jnp.float32)[:, None] * frequency[None, :]
    cosine, sine = jnp.cos(angles), jnp.sin(angles)
    turned = jnp.stack(
        [jnp.concatenate([cosine, cosine], axis=1), jnp.concatenate([-sine, sine], axis=1)]
    )
    table = jnp.stack([turned, jnp.stack([jnp.ones_like(turned[0]), jnp.zeros_like(turned[0])])])

    base = (node - 1) * n_i * rows
    starts = doc_starts(boundaries, (node * n_i + me) * rows + inside) - base
    ids = jnp.stack([node, me, starts[0]] + where).astype(jnp.int32)
    starts = starts[:, None]
    bias = bias[None]

    def projected(chunk, pieces, slots):
        first_column, width = columns[chunk]
        return project(
            ids, loader_counts, normed, table, bias, pieces, first_column, width, slots, n_i
        )

    later = after(w_qkv, ids)
    arrived, normed, table, ids, starts, waiting = lax.optimization_barrier(
        (
            cross(cut(0)),
            normed,
            table,
            ids,
            starts,
            [cut(chunk, later) for chunk in range(1, len(columns))],
        )
    )
    crossing_value = cross(waiting[0])
    [key] = projected(0, spread(0, passed(0, arrived)), None)
    keys_held = around(key, [key] * (n_i - 1))

    crossing = cross(after(waiting[1], key))
    crossed, waiting, _ = lax.optimization_barrier((crossing_value, waiting, keys_held))
    [value] = projected(1, spread(1, passed(1, crossed)), None)
    values_held = around(value, [value] * (n_i - 1))
    stacked = jnp.stack(
        [jnp.concatenate(both, axis=1) for both in zip(keys_held, values_held)]
    )
    behind = from_behind(stacked, "outer")

    crossing, waiting, _ = lax.optimization_barrier((crossing, waiting, value))
    sent = [swapped(array, "outer") for array in crossing]
    first, crossing = lax.optimization_barrier((passed(2, crossing), cross(waiting[2])))
    outs = projected(2, spread(2, after(first, stacked), sent), slot_rows)
    slots = [around(outs[0], outs[1:])]
    second = passed(3, crossing)
    keys, values = reorder(
        ids, loader_counts, after(stacked, outs[0], second), behind, slot_rows + 16
    )
    sent = [swapped(array, "outer") for array in after(crossing, outs[0])]
    outs = projected(3, spread(3, after(second, slots[0][n_i // 2], keys), sent), slot_rows)
    slots.append(around(outs[0], outs[1:]))

    output = None
    at = 0
    for chunk, heads in enumerate(CHUNKS):
        output = attend(
            ids, loader_counts, starts, keys, values, slots[chunk], output, at, heads, TOGETHER[chunk]
        )
        at += heads
    return output


def solution(mesh):
    in_specs = (
        P(("groups", "outer", "inner"), None),
        P(),
        P("outer", None),
        P(),
        P("groups"),
        P("groups", None, None),
    )
    out_specs = P(("groups", "outer", "inner"), None)
    return jax.shard_map(
        on_device, mesh=mesh, in_specs=in_specs, out_specs=out_specs, check_vma=False
    )
```
